32 devices in a mesh: parts: 2 (over y), row: 4 (over z), col: 4 (over x, core).
Axes of the slice: x: 2, y: 2, z: 4, core: 2. Of those that a mesh axis runs over, the one named last changes fastest.
Arguments:
- latent: bfloat16 [256, 128, 320], P(('parts', 'row'), 'col'), parts along dimension 0, may hold values from -6 to 6
- hyper: bfloat16 [64, 32, 192], P(('parts', 'row'), 'col'), parts along dimension 0, may hold values from -6 to 6
- bounds: int32 [6], replicated, may hold values from 0 to 320, as said below
- hyper_weight: bfloat16 [3, 3, 192, 192], replicated, may hold values from -0.15625 to 0.15625
- prior_weight: bfloat16 [192, 640], replicated, may hold values from -0.4375 to 0.4375
- ctx_weight: bfloat16 [4, 320, 640], replicated, may hold values from -0.3125 to 0.3125
- chan_weight: bfloat16 [320, 640], replicated, may hold values from -0.3125 to 0.3125
- out_weight: bfloat16 [640, 640], replicated, may hold values from -0.25 to 0.25
Outputs:
- rate_map: float32 [256, 128], P(('parts', 'row'), 'col'), parts along dimension 0
- grad_latent: bfloat16 [256, 128, 320], P(('parts', 'row'), 'col'), parts along dimension 0
- grad_hyper: float32 [64, 32, 192], P(('parts', 'row'), 'col'), parts along dimension 0
The draws below stay inside these ranges and needn't reach their ends.
There are 2 independent parts, one for each index of `parts`. The reference program is written for one: setup_inputs(seed, part) draws one part's arguments, and reference() takes and returns one part's arrays. A program takes and returns all parts, laid end to end along the dimension named above; an argument that names none is the same for every part. Nothing has to cross between parts.
Inputs may be any that keep to these rules, and one draw needn't show every extreme that they name: bounds[0] is 0, bounds[5] is 320, and bounds rises strictly.
All inputs are finite; a program needn't handle non-finite values.
Results may differ from the reference program's by a relative error of at most 0.0061.
Values may be sent and summed in bfloat16 or wider, within the bound.
A program may use at most 64 MiB of HBM per device.

```python
import jax
import jax.numpy as jnp
from jax import lax

C = 320
ZC = 192
HID = 640
H = 128
W = 128
HZ = 32
WZ = 32


def draw_bounds(key, part):
    jitter = jax.random.randint(key, (4,), 0, C // 40 + 1).astype(jnp.int32)
    base = jnp.array([C // 20, C // 10, C // 5, 2 * C // 5], jnp.int32)
    start = jnp.zeros((1,), jnp.int32)
    final = jnp.full((1,), C, jnp.int32)
    return jnp.concatenate([start, base + jitter, final]).astype(jnp.int32)


def block_levels(own_key, shape, cuts, least, top_value):
    level = 1.0
    for position, blocks in cuts:
        draws = jax.random.uniform(jax.random.fold_in(jax.random.fold_in(own_key, 6), position), (blocks,), jnp.float32, least / len(cuts), top_value / len(cuts))
        level = level * jnp.repeat(jnp.exp(draws), shape[position] // blocks).reshape((-1,) + (1,) * (len(shape) - 1 - position))
    return level


def scatter_about(key, shape, scale, most, cuts=(), held_as=jnp.bfloat16):
    values = scale * jax.random.normal(key, shape, jnp.float32)
    if cuts:
        values = values * block_levels(key, shape, cuts, -0.22, 0.18)
    return jnp.clip(values, -most, most).astype(held_as)


def setup_inputs(seed: int = 0, part: int = 0) -> dict:
    streams_of = jax.random.split(jax.random.key(seed), 9)
    own_keys = jax.random.split(jax.random.fold_in(streams_of[8], part), 9)
    return {
        "latent": scatter_about(own_keys[0], (H, W, C), 1.0, 6.0, ((0, 4), (1, 4))),
        "hyper": scatter_about(own_keys[1], (HZ, WZ, ZC), 1.0, 6.0, ((0, 4), (1, 4))),
        "bounds": draw_bounds(jax.random.fold_in(streams_of[8], 71), part),
        "hyper_weight": scatter_about(streams_of[3], (3, 3, ZC, ZC), (9 * ZC) ** -0.5, 0.15625),
        "prior_weight": scatter_about(streams_of[4], (ZC, HID), ZC ** -0.5, 0.4375),
        "ctx_weight": scatter_about(streams_of[5], (4, C, HID), C ** -0.5, 0.3125),
        "chan_weight": scatter_about(streams_of[6], (C, HID), C ** -0.5, 0.3125),
        "out_weight": scatter_about(streams_of[7], (HID, 2 * C), HID ** -0.5, 0.25),
    }


def slice_ids(bounds, channels):
    chan = jnp.arange(channels, dtype=jnp.int32)
    ids = jnp.zeros((channels,), jnp.int32)
    for g in range(1, 5):
        ids = ids + (chan >= bounds[g]).astype(jnp.int32)
    return ids

def silu_grad(value):
    sig = jax.nn.sigmoid(value)
    return sig * (1.0 + value * (1.0 - sig))

def reference(latent, hyper, bounds, hyper_weight, prior_weight, ctx_weight, chan_weight, out_weight):
    height, width, channels = latent.shape
    zrows, zcols, zch = hyper.shape
    hidden_units = prior_weight.shape[1]
    ids = slice_ids(bounds, channels)
    hid_ids = jnp.tile(ids, hidden_units // channels)
    par_ids = jnp.tile(ids, 2)
    same_mask = (ids[:, None] == hid_ids[None, :]).astype(jnp.bfloat16)
    prev_mask = (ids[:, None] < hid_ids[None, :]).astype(jnp.bfloat16)
    out_mask = (hid_ids[:, None] == par_ids[None, :]).astype(jnp.bfloat16)
    ctx_masked = ctx_weight * same_mask[None]
    chan_masked = chan_weight * prev_mask
    out_masked = out_weight * out_mask
    zpad = jnp.pad(hyper, ((1, 1), (1, 1), (0, 0)))
    taps = jnp.concatenate([zpad[a:a + zrows, b:b + zcols] for a in range(3) for b in range(3)], axis=-1)
    hz = jnp.dot(taps.reshape(-1, 9 * zch), hyper_weight.reshape(9 * zch, zch), preferred_element_type=jnp.float32)
    hfeat = jax.nn.silu(hz).astype(jnp.bfloat16).reshape(zrows, zcols, zch)
    hup = jnp.repeat(jnp.repeat(hfeat, 4, axis=0), 4, axis=1).reshape(-1, zch)
    rows_idx = jnp.arange(height, dtype=jnp.int32)
    cols_idx = jnp.arange(width, dtype=jnp.int32)
    anchor = (rows_idx[:, None] + cols_idx[None, :]) % 2 == 0
    ya = jnp.where(anchor[..., None], latent, jnp.zeros_like(latent))
    ypad = jnp.pad(ya, ((1, 1), (1, 1), (0, 0)))
    stacked = jnp.stack([ypad[0:height, 1:-1], ypad[2:, 1:-1], ypad[1:-1, 0:width], ypad[1:-1, 2:]], axis=2)
    stacked = stacked.reshape(-1, 4, channels)
    ctx = jnp.einsum('nkc,kch->nh', stacked.astype(jnp.float32), ctx_masked.astype(jnp.float32))
    flat = latent.reshape(-1, channels)
    pre = jnp.dot(hup, prior_weight, preferred_element_type=jnp.float32) + ctx
    pre = pre + jnp.dot(flat, chan_masked, preferred_element_type=jnp.float32)
    hidden = jax.nn.silu(pre).astype(jnp.bfloat16)
    par = jnp.dot(hidden, out_masked, preferred_element_type=jnp.float32)
    mu = par[:, :channels]
    sraw = par[:, channels:]
    sigma = 0.11 + jax.nn.softplus(sraw)
    resid = (flat.astype(jnp.float32) - mu) / sigma
    nll = 0.5 * resid * resid + jnp.log(sigma)
    rate_map = lax.optimization_barrier(jnp.mean(nll, axis=-1)).reshape(height, width)
    g_mu = -resid / sigma
    g_sraw = (1.0 - resid * resid) / sigma * jax.nn.sigmoid(sraw)
    g_par = jnp.concatenate([g_mu, g_sraw], axis=-1).astype(jnp.bfloat16)
    g_hidden = jnp.dot(g_par, out_masked.T, preferred_element_type=jnp.float32)
    g_pre = (g_hidden * silu_grad(pre)).astype(jnp.bfloat16)
    g_grid = g_pre.reshape(height, width, hidden_units)
    gpad = jnp.pad(g_grid, ((1, 1), (1, 1), (0, 0)))
    gstack = jnp.stack([gpad[2:, 1:-1], gpad[0:height, 1:-1], gpad[1:-1, 2:], gpad[1:-1, 0:width]], axis=2)
    gstack = gstack.reshape(-1, 4, hidden_units)
    spatial = jnp.einsum('nkh,kch->nc', gstack.astype(jnp.float32), ctx_masked.astype(jnp.float32))
    chan_back = jnp.dot(g_pre, chan_masked.T, preferred_element_type=jnp.float32)
    anchor_flat = anchor.reshape(-1, 1).astype(jnp.float32)
    grad_latent = (resid / sigma + chan_back + anchor_flat * spatial).astype(jnp.bfloat16)
    grad_latent = grad_latent.reshape(height, width, channels)
    g_hup = jnp.dot(g_pre, prior_weight.T, preferred_element_type=jnp.float32)
    g_h = g_hup.reshape(zrows, 4, zcols, 4, zch).sum(axis=(1, 3)).reshape(-1, zch)
    g_hz = (g_h * silu_grad(hz)).astype(jnp.bfloat16).reshape(zrows, zcols, zch)
    gzpad = jnp.pad(g_hz, ((1, 1), (1, 1), (0, 0)))
    gtaps = jnp.stack([gzpad[2 - a:2 - a + zrows, 2 - b:2 - b + zcols] for a in range(3) for b in range(3)], axis=2)
    gtaps = gtaps.reshape(-1, 9, zch)
    grad_hyper = jnp.einsum('nkz,kcz->nc', gtaps.astype(jnp.float32), hyper_weight.reshape(9, zch, zch).astype(jnp.float32))
    grad_hyper = grad_hyper.reshape(zrows, zcols, zch)
    return (rate_map, grad_latent, grad_hyper)
```

```python
import jax
import jax.numpy as jnp
import numpy as np
from jax import lax
from jax.experimental import pallas as pl
from jax.experimental.pallas import tpu as pltpu
from jax.sharding import PartitionSpec as P

BF = jnp.bfloat16
F32 = jnp.float32
DIRS = ((-1, 0), (1, 0), (0, -1), (0, 1), (-1, -1), (-1, 1), (1, -1), (1, 1))
OPP = (1, 0, 3, 2, 7, 6, 5, 4)


def dot(a, b):
    return jnp.dot(a, b, preferred_element_type=F32)


def dot_t(a, b):
    return lax.dot_general(a, b, (((1,), (1,)), ((), ())), preferred_element_type=F32)


def tables(rows, cols, zrows, zcols, tr):
    half = cols // 2
    sub = 8
    m = np.arange(sub * half)
    ir, k = m // half, m % half
    ps = np.zeros((3 * sub * half, sub * cols), np.float32)
    n = sub * half
    ps[m, ir * cols + 2 * k + ir % 2] = 1
    ps[n + m, ir * cols + 2 * k + 1 - ir % 2] = 1
    for q in m:
        kk = k[q] + (1 if ir[q] % 2 == 0 else -1)
        if 0 <= kk < half:
            ps[2 * n + q, ir[q] * cols + 2 * kk + ir[q] % 2] = 1
    pt = ps[: 2 * n].T.copy()
    m = np.arange(tr * half)
    ir, k = m // half, m % half
    sb = np.zeros((tr * half, tr * half), np.float32)
    for q in m:
        kk = k[q] + (-1 if ir[q] % 2 == 0 else 1)
        if 0 <= kk < half:
            sb[q, ir[q] * half + kk] = 1
    m = np.arange(rows * half)
    i, k = m // half, m % half
    up = np.zeros((rows * half, zrows * zcols), np.float32)
    up[m, (i // 4) * zcols + k // 2] = 1
    qf = np.zeros((rows * half, rows), np.float32)
    qb = np.zeros((rows * half, rows), np.float32)
    ef = np.zeros((rows, rows * half), np.float32)
    eb = np.zeros((rows, rows * half), np.float32)
    for r in range(rows):
        e = r // 2 + (rows // 2 if r % 2 else 0)
        qf[r * half + (half - 1 if r % 2 == 0 else 0), e] = 1
        qb[r * half + (0 if r % 2 == 0 else half - 1), e] = 1
        ef[e, r * half + (0 if r % 2 == 0 else half - 1)] = 1
        eb[e, r * half + (half - 1 if r % 2 == 0 else 0)] = 1
    cells = zrows * zcols
    tz = np.zeros((9 * cells, cells + 8 * 16), np.float32)
    for a in range(3):
        for b in range(3):
            for zi in range(zrows):
                for zj in range(zcols):
                    y, x = zi + a - 1, zj + b - 1
                    dr = -1 if y < 0 else (1 if y >= zrows else 0)
                    dc = -1 if x < 0 else (1 if x >= zcols else 0)
                    if (dr, dc) == (0, 0):
                        s = y * zcols + x
                    else:
                        s = cells + 16 * DIRS.index((dr, dc))
                        if dr == 0:
                            s += y
                        else:
                            s += (16 - zcols if dr < 0 else 0) + x % zcols
                    tz[(a * 3 + b) * cells + zi * zcols + zj, s] = 1
    ez = np.zeros((32, cells), np.float32)
    for zi in range(zrows):
        ez[zi, zi * zcols] = 1
        ez[16 + zi, zi * zcols + zcols - 1] = 1
    m = np.arange(tr * half)
    ir, k = m // half, m % half
    w = tr * half
    rg = np.zeros((tr, 2 * w), np.float32)
    rg[ir, m] = 1
    rg[ir, w + m] = 1
    cm = np.zeros((2 * w, cols), np.float32)
    cm[m, 2 * k + ir % 2] = 1
    cm[w + m, 2 * k + 1 - ir % 2] = 1
    return [x.astype(jnp.bfloat16) for x in (ps, pt, sb, up, up.T.copy(), qf, qb, ef, eb, tz, ez, rg, cm)]


def make_kernel(rows, cols, ch, zrows, zcols, zch, hid, tr, nrow, ncol):
    half = cols // 2
    full = (ch // 256) * 256
    rem = ch - full
    cp = full + 2 * rem
    cells = zrows * zcols
    w = tr * half
    tiles = rows // tr
    own = rows * half

    def kernel(*refs):
        (bounds, latent, hyper, hw_in, pw_in, cw_in, kw_in, ow_in, *tabs) = refs[:21]
        rate_out, gl_out, gh_out = refs[21:24]
        (lat, hw, wt, owr, wo, ps, pt, sb, up, upt, qf, qb, ef, eb, tz, ez, rg, cm,
         ae, nn, ss, hcf, csf, he, csh, gne, ga, rs, hcb, csb, gz, csz, in_sem, send_sem, recv_sem) = refs[24:]
        tab_v = (ps, pt, sb, up, upt, qf, qb, ef, eb, tz, ez, rg, cm)
        my_r = lax.axis_index("row")
        my_c = lax.axis_index("col")

        def there(d):
            dr, dc = DIRS[d]
            ok = my_r >= 0
            if dr < 0:
                ok = my_r > 0
            if dr > 0:
                ok = my_r < nrow - 1
            if dc < 0:
                ok = ok & (my_c > 0)
            if dc > 0:
                ok = ok & (my_c < ncol - 1)
            return ok

        def dev(d):
            return {"row": my_r + DIRS[d][0], "col": my_c + DIRS[d][1]}

        barrier = pltpu.get_barrier_semaphore()
        for d in range(8):
            @pl.when(there(d))
            def _(d=d):
                pl.semaphore_signal(barrier, inc=1, device_id=dev(d), device_id_type=pl.DeviceIdType.MESH)

        loads = []

        def load(src, dst):
            c = pltpu.make_async_copy(src, dst, in_sem.at[len(loads)])
            c.start()
            loads.append(c)
            return len(loads) - 1

        ld_lat = load(latent, lat)
        ld_hyper = load(hyper, he.at[pl.ds(0, cells)])
        ld_tab = [load(a, b) for a, b in zip(tabs, tab_v)]
        ld_hw = load(hw_in, hw)
        ld_w = []
        for d in range(4):
            ld_w.append(load(cw_in.at[pl.ds(d * ch, full)], wt.at[pl.ds(d * full, full)]))
            ld_w.append(load(cw_in.at[pl.ds(d * ch + full, rem)], wt.at[pl.ds(5 * full + d * rem, rem)]))
        ld_w.append(load(kw_in.at[pl.ds(0, full)], wt.at[pl.ds(4 * full, full)]))
        ld_w.append(load(kw_in.at[pl.ds(full, rem)], wt.at[pl.ds(5 * full + 4 * rem, rem)]))
        ld_w.append(load(pw_in.at[pl.ds(128, zch - 128)], wt.at[pl.ds(5 * ch, zch - 128)]))
        ld_w.append(load(pw_in.at[pl.ds(0, 128)], wt.at[pl.ds(5 * ch + zch - 128, 128)]))
        ld_ow = load(ow_in, owr)

        def absent(d, fill):
            @pl.when(jnp.logical_not(there(d)))
            def _():
                fill()

        def zero(ref, start, size):
            def fill():
                ref[pl.ds(start, size), :] = jnp.zeros((size, ref.shape[1]), ref.dtype)
            return fill

        for d in range(8):
            absent(d, zero(he, cells + 16 * d, 16))
            absent(d, zero(gz, cells + 16 * d, 16))
        absent(0, zero(ae, 0, half))
        absent(1, zero(ae, half + own, half))
        absent(0, zero(gne, 0, half))
        absent(1, zero(gne, half + own, half))
        hr = rows // 2
        absent(3, zero(hcf, 0, hr))
        absent(2, zero(hcf, hr, hr))
        absent(2, zero(hcb, 0, hr))
        absent(3, zero(hcb, hr, hr))

        def remote(idx, d, src, dst):
            return pltpu.make_async_remote_copy(
                src_ref=src, dst_ref=dst, send_sem=send_sem.at[idx], recv_sem=recv_sem.at[idx],
                device_id=dev(d), device_id_type=pl.DeviceIdType.MESH)

        def hyper_copies(base, ext, col):
            out = []
            for d, (dr, dc) in enumerate(DIRS):
                if dr < 0:
                    src = ext.at[pl.ds(0, 16)]
                elif dr > 0:
                    src = ext.at[pl.ds(cells - 16, 16)]
                else:
                    src = col.at[pl.ds(0 if dc < 0 else 16, 16)]
                out.append((d, OPP[d], remote(base + OPP[d], d, src, ext.at[pl.ds(cells + 16 * OPP[d], 16)])))
            return out

        def side_copies(base, ext, col, halo, left_first):
            lf = 0 if left_first else hr
            rf = hr - lf
            return [
                (0, 1, remote(base + 1, 0, ext.at[pl.ds(half, half)], ext.at[pl.ds(half + own, half)])),
                (1, 0, remote(base + 0, 1, ext.at[pl.ds(own, half)], ext.at[pl.ds(0, half)])),
                (2, 3, remote(base + 3, 2, col.at[pl.ds(lf, hr)], halo.at[pl.ds(lf, hr)])),
                (3, 2, remote(base + 2, 3, col.at[pl.ds(rf, hr)], halo.at[pl.ds(rf, hr)])),
            ]

        hyper_c = hyper_copies(0, he, csh)
        lat_c = side_copies(8, ae, csf, hcf, True)
        gpre_c = side_copies(12, gne, csb, hcb, False)
        gz_c = hyper_copies(16, gz, csz)

        def start(copies):
            for d, _, c in copies:
                @pl.when(there(d))
                def _(c=c):
                    c.start()

        def wait_recv(copies):
            for _, o, c in copies:
                @pl.when(there(o))
                def _(c=c):
                    c.wait_recv()

        def wait_send(copies):
            for d, _, c in copies:
                @pl.when(there(d))
                def _(c=c):
                    c.wait_send()

        loads[ld_lat].wait()
        loads[ld_hyper].wait()
        for i in ld_tab:
            loads[i].wait()
        csh[...] = dot(ez[...], he[pl.ds(0, cells), :]).astype(BF)
        n8 = 8 * half
        for t in range(rows // 8):
            y = dot(ps[...], lat[pl.ds(t * 8 * cols, 8 * cols), :])
            y = jnp.concatenate([y[:, :full], y[:, full:], y[:, full:]], axis=1).astype(BF)
            ae[pl.ds(half + t * n8, n8), :] = y[:n8]
            nn[pl.ds(t * n8, n8), :] = y[n8 : 2 * n8]
            ss[pl.ds(t * n8, n8), :] = y[2 * n8 :]
        csf[...] = dot(ef[...], ae[pl.ds(half, own), :]).astype(BF)

        count = jnp.int32(0)
        for d in range(8):
            count = count + there(d).astype(jnp.int32)
        pl.semaphore_wait(barrier, count)
        start(hyper_c)
        start(lat_c)

        def ids(shape, dim, period, width):
            c = lax.broadcasted_iota(jnp.int32, shape, dim)
            c = jnp.where(c >= period, c - period, c)
            s = jnp.zeros(shape, jnp.int32)
            for g in range(1, 5):
                s = s + (c >= bounds[g]).astype(jnp.int32)
            return jnp.where(c < width, s, -1)

        col_id = ids((1, hid), 1, ch, ch)
        row_id = ids((ch, 1), 0, ch, ch)
        same = jnp.where(row_id == col_id, 1.0, 0.0).astype(BF)
        prev = jnp.where(row_id < col_id, 1.0, 0.0).astype(BF)
        for i in ld_w:
            loads[i].wait()
        for d in range(5):
            mask = prev if d == 4 else same
            a = pl.ds(d * full, full)
            wt[a, :] = wt[a, :] * mask[:full]
            b = pl.ds(5 * full + d * rem, rem)
            wt[b, :] = wt[b, :] * mask[full:]
        hid_id = ids((hid, 1), 0, ch, ch)
        par_id = ids((1, 2 * cp), 1, cp, ch)
        omask = jnp.where(hid_id == par_id, 1.0, 0.0).astype(BF)
        loads[ld_ow].wait()
        raw = owr[...].astype(F32)
        pad = jnp.zeros((hid, cp - ch), F32)
        wide = jnp.concatenate([raw[:, :ch], pad, raw[:, ch:], pad], axis=1).astype(BF)
        wo[...] = wide * omask

        loads[ld_hw].wait()
        wait_recv(hyper_c)
        taps = dot(tz[...], he[...]).astype(BF)
        hz = jnp.zeros((cells, zch), F32)
        for ab in range(9):
            hz = hz + dot(taps[ab * cells : (ab + 1) * cells], hw[pl.ds(ab * zch, zch), :])
        sz = jax.nn.sigmoid(hz)
        dz = sz * (1.0 + hz * (1.0 - sz))
        f = hz * sz
        feat = jnp.concatenate([jnp.zeros((cells, rem), F32), f[:, 128:], f[:, :128]], axis=1).astype(BF)
        wait_recv(lat_c)

        def mix(even, odd):
            return jnp.concatenate(
                [(even if i % 2 == 0 else odd)[i * half : (i + 1) * half] for i in range(tr)], axis=0)

        lane = lax.broadcasted_iota(jnp.int32, (w, 2 * rem), 1)
        left = lane < rem

        def pair(a, b):
            return jnp.where(left, a, b)

        kidx = lax.broadcasted_iota(jnp.int32, (2 * w, cp), 1)
        gsum = jnp.zeros((cells, hid), F32)
        for t in range(tiles):
            at = t * w
            a = ae[pl.ds(half + at, w), :]
            au = ae[pl.ds(at, w), :]
            ad = ae[pl.ds(2 * half + at, w), :]
            o = nn[pl.ds(at, w), :]
            s = (ss[pl.ds(at, w), :].astype(F32) + dot(qf[pl.ds(at, w), :], hcf[...])).astype(BF)
            al = mix(a, s)
            ar = mix(s, a)
            hup = dot(up[pl.ds(at, w), :], feat).astype(BF)
            h0, h1 = hup[:, : 2 * rem], hup[:, 2 * rem :]
            x = jnp.concatenate(
                [au[:, :full], ad[:, :full], al[:, :full], ar[:, :full], o[:, :full],
                 pair(au[:, full:], ad[:, full:]), pair(al[:, full:], ar[:, full:]),
                 pair(o[:, full:], h0), h1], axis=1)
            pre_n = dot(x, wt[...])
            xa = jnp.concatenate([pair(a[:, full:], h0), h1], axis=1)
            pre_a = dot(a[:, :full], wt[pl.ds(4 * full, full), :]) + dot(
                xa, wt[pl.ds(5 * full + 4 * rem, rem + zch), :])
            pre = jnp.concatenate([pre_a, pre_n], axis=0)
            sg = 0.5 * jnp.tanh(0.5 * pre) + 0.5
            hidden = pre * sg
            ds = sg + hidden * (1.0 - sg)
            par = dot(hidden.astype(BF), wo[...])
            mu = par[:, :cp]
            sraw = par[:, cp:]
            e = jnp.exp(-jnp.abs(sraw))
            sigma = 0.11 + (jnp.maximum(sraw, 0.0) + jnp.log(1.0 + e))
            inv = 1.0 / sigma
            y = jnp.concatenate([a, o], axis=0).astype(F32)
            r = (y - mu) * inv
            nll = 0.5 * r * r + jnp.log(sigma)
            rate = jnp.sum(jnp.where(kidx < ch, nll, 0.0), axis=1, keepdims=True) * (1.0 / ch)
            spread = rate * cm[...].astype(F32)
            hi = spread.astype(BF)
            lo = (spread - hi.astype(F32)).astype(BF)
            rate_out[pl.ds(t * tr, tr), :] = dot(rg[...], hi) + dot(rg[...], lo)
            rsig = r * inv
            rs[pl.ds(2 * at, 2 * w), :] = rsig
            sgs = jnp.where(sraw >= 0.0, 1.0, e) / (1.0 + e)
            g_par = jnp.concatenate([-rsig, (1.0 - r * r) * inv * sgs], axis=1).astype(BF)
            gp = (dot_t(g_par, wo[...]) * ds).astype(BF)
            ga[pl.ds(at, w), :] = gp[:w]
            gne[pl.ds(half + at, w), :] = gp[w:]
            ut = upt[:, at : at + w]
            gsum = gsum + dot(ut, gp[:w]) + dot(ut, gp[w:])

        csb[...] = dot(eb[...], gne[pl.ds(half, own), :]).astype(BF)
        start(gpre_c)

        hi = gsum.astype(BF)
        lo = (gsum - hi.astype(F32)).astype(BF)
        both = jnp.concatenate([hi, lo], axis=0)
        p0 = dot_t(both, wt[pl.ds(5 * ch + zch - 128, 128), :])
        p1 = dot_t(both, wt[pl.ds(5 * ch, zch - 128), :])
        g_h = jnp.concatenate([p0[:cells] + p0[cells:], p1[:cells] + p1[cells:]], axis=1)
        g_hz = (g_h * dz).astype(BF)
        gz[pl.ds(0, cells), :] = g_hz
        csz[...] = dot(ez[...], g_hz).astype(BF)
        start(gz_c)

        wait_recv(gpre_c)
        wcm = wt[pl.ds(4 * full, full), :]
        wcr = wt[pl.ds(5 * full + 4 * rem, rem), :]
        for t in range(tiles):
            at = t * w
            gn = gne[pl.ds(half + at, w), :]
            gu = gne[pl.ds(at, w), :]
            gd = gne[pl.ds(2 * half + at, w), :]
            s = (dot(sb[...], gn) + dot(qb[pl.ds(at, w), :], hcb[...])).astype(BF)
            gr = mix(gn, s)
            gl = mix(s, gn)
            gs = (gd, gu, gr, gl, ga[pl.ds(at, w), :])
            m = rs[pl.ds(2 * at, w), :full]
            q = rs[pl.ds(2 * at, w), full:ch]
            for d in range(5):
                m = m + dot_t(gs[d], wt[pl.ds(d * full, full), :])
                q = q + dot_t(gs[d], wt[pl.ds(5 * full + d * rem, rem), :])
            nm = rs[pl.ds(2 * at + w, w), :full] + dot_t(gn, wcm)
            nq = rs[pl.ds(2 * at + w, w), full:ch] + dot_t(gn, wcr)
            va = jnp.concatenate([m, q], axis=1).astype(BF)
            vn = jnp.concatenate([nm, nq], axis=1).astype(BF)
            for u in range(tr // 8):
                v = jnp.concatenate([va[u * n8 : (u + 1) * n8], vn[u * n8 : (u + 1) * n8]], axis=0)
                gl_out[pl.ds((t * tr + u * 8) * cols, 8 * cols), :] = dot(pt[...], v).astype(BF)

        wait_recv(gz_c)
        taps = dot(tz[...], gz[...]).astype(BF)
        acc = jnp.zeros((cells, zch), F32)
        for ab in range(9):
            back = 8 - ab
            acc = acc + dot_t(taps[back * cells : (back + 1) * cells], hw[pl.ds(ab * zch, zch), :])
        gh_out[...] = acc

        wait_send(hyper_c)
        wait_send(lat_c)
        wait_send(gpre_c)
        wait_send(gz_c)

    return kernel


def solution(mesh):
    nrow, ncol = mesh.shape["row"], mesh.shape["col"]

    def local(latent, hyper, bounds, hyper_weight, prior_weight, ctx_weight, chan_weight, out_weight):
        rows, cols, ch = latent.shape
        zrows, zcols, zch = hyper.shape
        hid = prior_weight.shape[1]
        tr = 16
        half = cols // 2
        full = (ch // 256) * 256
        rem = ch - full
        cp = full + 2 * rem
        cells = zrows * zcols
        own = rows * half
        tabs = tables(rows, cols, zrows, zcols, tr)
        hr = rows // 2
        anyspec = pl.BlockSpec(memory_space=pl.ANY)
        vm = pl.BlockSpec(memory_space=pltpu.VMEM)
        v = lambda *s, dt=BF: pltpu.VMEM(s, dt)
        scratch = [
            v(rows * cols, ch), v(9 * zch, zch), v(5 * ch + zch, hid), v(hid, hid), v(hid, 2 * cp),
            *[v(*t.shape) for t in tabs],
            v(own + 2 * half, cp), v(own, cp), v(own, cp), v(2 * hr, cp), v(2 * hr, cp),
            v(cells + 128, zch), v(32, zch),
            v(own + 2 * half, hid), v(own, hid), v(rows * cols, cp, dt=F32), v(2 * hr, hid), v(2 * hr, hid),
            v(cells + 128, zch), v(32, zch),
            pltpu.SemaphoreType.DMA((32,)), pltpu.SemaphoreType.DMA((24,)), pltpu.SemaphoreType.DMA((24,)),
        ]
        rate, gl, gh = pl.pallas_call(
            make_kernel(rows, cols, ch, zrows, zcols, zch, hid, tr, nrow, ncol),
            out_shape=(
                jax.ShapeDtypeStruct((rows, cols), F32),
                jax.ShapeDtypeStruct((rows * cols, ch), BF),
                jax.ShapeDtypeStruct((cells, zch), F32),
            ),
            in_specs=[pl.BlockSpec(memory_space=pltpu.SMEM)] + [anyspec] * (7 + len(tabs)),
            out_specs=(vm, vm, vm),
            scratch_shapes=scratch,
            compiler_params=pltpu.CompilerParams(
                collective_id=0, has_side_effects=True, vmem_limit_bytes=56 * 1024 * 1024),
        )(
            bounds, latent.reshape(rows * cols, ch), hyper.reshape(cells, zch),
            hyper_weight.reshape(9 * zch, zch), prior_weight, ctx_weight.reshape(4 * ch, hid),
            chan_weight, out_weight, *[jnp.asarray(t) for t in tabs],
        )
        return rate, gl.reshape(rows, cols, ch), gh.reshape(zrows, zcols, zch)

    in_specs = (
        P(("parts", "row"), "col", None),
        P(("parts", "row"), "col", None),
        P(),
        P(),
        P(),
        P(),
        P(),
        P(),
    )
    out_specs = (
        P(("parts", "row"), "col"),
        P(("parts", "row"), "col", None),
        P(("parts", "row"), "col", None),
    )
    return jax.shard_map(local, mesh=mesh, in_specs=in_specs, out_specs=out_specs, check_vma=False)
```

```python
import jax
import jax.numpy as jnp
import numpy as np
from jax import lax
from jax.experimental import pallas as pl
from jax.experimental.pallas import tpu as pltpu
from jax.sharding import PartitionSpec as P

BF = jnp.bfloat16
F32 = jnp.float32
DIRS = ((-1, 0), (1, 0), (0, -1), (0, 1), (-1, -1), (-1, 1), (1, -1), (1, 1))
OPP = (1, 0, 3, 2, 7, 6, 5, 4)


def dot(a, b):
    return jnp.dot(a, b, preferred_element_type=F32)


def dot_t(a, b):
    return lax.dot_general(a, b, (((1,), (1,)), ((), ())), preferred_element_type=F32)


def tables(rows, cols, zrows, zcols, tr):
    half = cols // 2
    sub = 8
    m = np.arange(sub * half)
    ir, k = m // half, m % half
    ps = np.zeros((3 * sub * half, sub * cols), np.float32)
    n = sub * half
    ps[m, ir * cols + 2 * k + ir % 2] = 1
    ps[n + m, ir * cols + 2 * k + 1 - ir % 2] = 1
    for q in m:
        kk = k[q] + (1 if ir[q] % 2 == 0 else -1)
        if 0 <= kk < half:
            ps[2 * n + q, ir[q] * cols + 2 * kk + ir[q] % 2] = 1
    pt = ps[: 2 * n].T.copy()
    m = np.arange(tr * half)
    ir, k = m // half, m % half
    sb = np.zeros((tr * half, tr * half), np.float32)
    for q in m:
        kk = k[q] + (-1 if ir[q] % 2 == 0 else 1)
        if 0 <= kk < half:
            sb[q, ir[q] * half + kk] = 1
    m = np.arange(rows * half)
    i, k = m // half, m % half
    up = np.zeros((rows * half, zrows * zcols), np.float32)
    up[m, (i // 4) * zcols + k // 2] = 1
    qf = np.zeros((rows * half, rows), np.float32)
    qb = np.zeros((rows * half, rows), np.float32)
    ef = np.zeros((rows, rows * half), np.float32)
    eb = np.zeros((rows, rows * half), np.float32)
    for r in range(rows):
        e = r // 2 + (rows // 2 if r % 2 else 0)
        qf[r * half + (half - 1 if r % 2 == 0 else 0), e] = 1
        qb[r * half + (0 if r % 2 == 0 else half - 1), e] = 1
        ef[e, r * half + (0 if r % 2 == 0 else half - 1)] = 1
        eb[e, r * half + (half - 1 if r % 2 == 0 else 0)] = 1
    cells = zrows * zcols
    tz = np.zeros((9 * cells, cells + 8 * 16), np.float32)
    for a in range(3):
        for b in range(3):
            for zi in range(zrows):
                for zj in range(zcols):
                    y, x = zi + a - 1, zj + b - 1
                    dr = -1 if y < 0 else (1 if y >= zrows else 0)
                    dc = -1 if x < 0 else (1 if x >= zcols else 0)
                    if (dr, dc) == (0, 0):
                        s = y * zcols + x
                    else:
                        s = cells + 16 * DIRS.index((dr, dc))
                        if dr == 0:
                            s += y
                        else:
                            s += (16 - zcols if dr < 0 else 0) + x % zcols
                    tz[(a * 3 + b) * cells + zi * zcols + zj, s] = 1
    ez = np.zeros((32, cells), np.float32)
    for zi in range(zrows):
        ez[zi, zi * zcols] = 1
        ez[16 + zi, zi * zcols + zcols - 1] = 1
    m = np.arange(tr * half)
    ir, k = m // half, m % half
    w = tr * half
    rg = np.zeros((tr, 2 * w), np.float32)
    rg[ir, m] = 1
    rg[ir, w + m] = 1
    cm = np.zeros((2 * w, cols), np.float32)
    cm[m, 2 * k + ir % 2] = 1
    cm[w + m, 2 * k + 1 - ir % 2] = 1
    return [x.astype(jnp.bfloat16) for x in (ps, pt, sb, up, up.T.copy(), qf, qb, ef, eb, tz, ez, rg, cm)]


def make_kernel(rows, cols, ch, zrows, zcols, zch, hid, tr, nrow, ncol):
    half = cols // 2
    full = (ch // 256) * 256
    rem = ch - full
    cp = full + 2 * rem
    cells = zrows * zcols
    w = tr * half
    tiles = rows // tr
    own = rows * half

    def kernel(*refs):
        (bounds, latent, hyper, hw_in, pw_in, cw_in, kw_in, ow_in, *tabs) = refs[:21]
        rate_out, gl_out, gh_out = refs[21:24]
        (lat, hw, wt, owr, wo, ps, pt, sb, up, upt, qf, qb, ef, eb, tz, ez, rg, cm,
         ae, nn, ss, hcf, csf, he, csh, gne, ga, rs, hcb, csb, gz, csz, rate_v, gl_v, gh_v,
         in_sem, out_sem, send_sem, recv_sem) = refs[24:]
        tab_v = (ps, pt, sb, up, upt, qf, qb, ef, eb, tz, ez, rg, cm)
        my_r = lax.axis_index("row")
        my_c = lax.axis_index("col")

        def there(d):
            dr, dc = DIRS[d]
            ok = my_r >= 0
            if dr < 0:
                ok = my_r > 0
            if dr > 0:
                ok = my_r < nrow - 1
            if dc < 0:
                ok = ok & (my_c > 0)
            if dc > 0:
                ok = ok & (my_c < ncol - 1)
            return ok

        def dev(d):
            return {"row": my_r + DIRS[d][0], "col": my_c + DIRS[d][1]}

        barrier = pltpu.get_barrier_semaphore()
        for d in range(8):
            @pl.when(there(d))
            def _(d=d):
                pl.semaphore_signal(barrier, inc=1, device_id=dev(d), device_id_type=pl.DeviceIdType.MESH)

        loads = []

        def load(src, dst):
            c = pltpu.make_async_copy(src, dst, in_sem.at[len(loads)])
            c.start()
            loads.append(c)
            return len(loads) - 1

        ld_lat = load(latent, lat)
        ld_hyper = load(hyper, he.at[pl.ds(0, cells)])
        early = (0, 7, 10)
        ld_early = [load(tabs[i], tab_v[i]) for i in early]
        ld_w = []
        for d in range(4):
            ld_w.append(load(cw_in.at[pl.ds(d * ch, full)], wt.at[pl.ds(d * full, full)]))
            ld_w.append(load(cw_in.at[pl.ds(d * ch + full, rem)], wt.at[pl.ds(5 * full + d * rem, rem)]))
        ld_w.append(load(kw_in.at[pl.ds(0, full)], wt.at[pl.ds(4 * full, full)]))
        ld_w.append(load(kw_in.at[pl.ds(full, rem)], wt.at[pl.ds(5 * full + 4 * rem, rem)]))
        ld_w.append(load(pw_in.at[pl.ds(128, zch - 128)], wt.at[pl.ds(5 * ch, zch - 128)]))
        ld_w.append(load(pw_in.at[pl.ds(0, 128)], wt.at[pl.ds(5 * ch + zch - 128, 128)]))
        ld_ow = load(ow_in, owr)
        ld_hw = load(hw_in, hw)
        ld_late = [load(tabs[i], tab_v[i]) for i in range(len(tabs)) if i not in early]

        def absent(d, fill):
            @pl.when(jnp.logical_not(there(d)))
            def _():
                fill()

        def zero(ref, start, size):
            def fill():
                ref[pl.ds(start, size), :] = jnp.zeros((size, ref.shape[1]), ref.dtype)
            return fill

        for d in range(8):
            absent(d, zero(he, cells + 16 * d, 16))
            absent(d, zero(gz, cells + 16 * d, 16))
        absent(0, zero(ae, 0, half))
        absent(1, zero(ae, half + own, half))
        absent(0, zero(gne, 0, half))
        absent(1, zero(gne, half + own, half))
        hr = rows // 2
        absent(3, zero(hcf, 0, hr))
        absent(2, zero(hcf, hr, hr))
        absent(2, zero(hcb, 0, hr))
        absent(3, zero(hcb, hr, hr))

        def remote(idx, d, src, dst):
            return pltpu.make_async_remote_copy(
                src_ref=src, dst_ref=dst, send_sem=send_sem.at[idx], recv_sem=recv_sem.at[idx],
                device_id=dev(d), device_id_type=pl.DeviceIdType.MESH)

        def hyper_copies(base, ext, col):
            out = []
            for d, (dr, dc) in enumerate(DIRS):
                if dr < 0:
                    src = ext.at[pl.ds(0, 16)]
                elif dr > 0:
                    src = ext.at[pl.ds(cells - 16, 16)]
                else:
                    src = col.at[pl.ds(0 if dc < 0 else 16, 16)]
                out.append((d, OPP[d], remote(base + OPP[d], d, src, ext.at[pl.ds(cells + 16 * OPP[d], 16)])))
            return out

        def side_copies(base, ext, col, halo, left_first):
            lf = 0 if left_first else hr
            rf = hr - lf
            return [
                (0, 1, remote(base + 1, 0, ext.at[pl.ds(half, half)], ext.at[pl.ds(half + own, half)])),
                (1, 0, remote(base + 0, 1, ext.at[pl.ds(own, half)], ext.at[pl.ds(0, half)])),
                (2, 3, remote(base + 3, 2, col.at[pl.ds(lf, hr)], halo.at[pl.ds(lf, hr)])),
                (3, 2, remote(base + 2, 3, col.at[pl.ds(rf, hr)], halo.at[pl.ds(rf, hr)])),
            ]

        hyper_c = hyper_copies(0, he, csh)
        lat_c = side_copies(8, ae, csf, hcf, True)
        gpre_c = side_copies(12, gne, csb, hcb, False)
        gz_c = hyper_copies(16, gz, csz)

        def start(copies):
            for d, _, c in copies:
                @pl.when(there(d))
                def _(c=c):
                    c.start()

        def wait_recv(copies):
            for _, o, c in copies:
                @pl.when(there(o))
                def _(c=c):
                    c.wait_recv()

        def wait_send(copies):
            for d, _, c in copies:
                @pl.when(there(d))
                def _(c=c):
                    c.wait_send()

        loads[ld_lat].wait()
        loads[ld_hyper].wait()
        for i in ld_early:
            loads[i].wait()
        csh[...] = dot(ez[...], he[pl.ds(0, cells), :]).astype(BF)
        n8 = 8 * half
        for t in range(rows // 8):
            y = dot(ps[...], lat[pl.ds(t * 8 * cols, 8 * cols), :])
            y = jnp.concatenate([y[:, :full], y[:, full:], y[:, full:]], axis=1).astype(BF)
            ae[pl.ds(half + t * n8, n8), :] = y[:n8]
            nn[pl.ds(t * n8, n8), :] = y[n8 : 2 * n8]
            ss[pl.ds(t * n8, n8), :] = y[2 * n8 :]
        csf[...] = dot(ef[...], ae[pl.ds(half, own), :]).astype(BF)

        count = jnp.int32(0)
        for d in range(8):
            count = count + there(d).astype(jnp.int32)
        pl.semaphore_wait(barrier, count)
        start(hyper_c)
        start(lat_c)

        def ids(shape, dim, period, width):
            c = lax.broadcasted_iota(jnp.int32, shape, dim)
            c = jnp.where(c >= period, c - period, c)
            s = jnp.zeros(shape, jnp.int32)
            for g in range(1, 5):
                s = s + (c >= bounds[g]).astype(jnp.int32)
            return jnp.where(c < width, s, -1)

        col_id = ids((1, hid), 1, ch, ch)
        row_id = ids((ch, 1), 0, ch, ch)
        same = jnp.where(row_id == col_id, 1.0, 0.0).astype(BF)
        prev = jnp.where(row_id < col_id, 1.0, 0.0).astype(BF)
        for i in ld_w:
            loads[i].wait()
        for d in range(5):
            mask = prev if d == 4 else same
            a = pl.ds(d * full, full)
            wt[a, :] = wt[a, :] * mask[:full]
            b = pl.ds(5 * full + d * rem, rem)
            wt[b, :] = wt[b, :] * mask[full:]
        hid_id = ids((hid, 1), 0, ch, ch)
        par_id = ids((1, 2 * cp), 1, cp, ch)
        omask = jnp.where(hid_id == par_id, 1.0, 0.0).astype(BF)
        loads[ld_ow].wait()
        raw = owr[...].astype(F32)
        pad = jnp.zeros((hid, cp - ch), F32)
        wide = jnp.concatenate([raw[:, :ch], pad, raw[:, ch:], pad], axis=1).astype(BF)
        wo[...] = wide * omask

        loads[ld_hw].wait()
        for i in ld_late:
            loads[i].wait()
        wait_recv(hyper_c)
        taps = dot(tz[...], he[...]).astype(BF)
        hz = jnp.zeros((cells, zch), F32)
        for ab in range(9):
            hz = hz + dot(taps[ab * cells : (ab + 1) * cells], hw[pl.ds(ab * zch, zch), :])
        sz = jax.nn.sigmoid(hz)
        dz = sz * (1.0 + hz * (1.0 - sz))
        f = hz * sz
        feat = jnp.concatenate([jnp.zeros((cells, rem), F32), f[:, 128:], f[:, :128]], axis=1).astype(BF)
        wait_recv(lat_c)

        def mix(even, odd):
            return jnp.concatenate(
                [(even if i % 2 == 0 else odd)[i * half : (i + 1) * half] for i in range(tr)], axis=0)

        lane = lax.broadcasted_iota(jnp.int32, (w, 2 * rem), 1)
        left = lane < rem

        def pair(a, b):
            return jnp.where(left, a, b)

        kidx = lax.broadcasted_iota(jnp.int32, (2 * w, cp), 1)

        def stage_pre(t):
            at = t * w
            a = ae[pl.ds(half + at, w), :]
            au = ae[pl.ds(at, w), :]
            ad = ae[pl.ds(2 * half + at, w), :]
            o = nn[pl.ds(at, w), :]
            s = (ss[pl.ds(at, w), :].astype(F32) + dot(qf[pl.ds(at, w), :], hcf[...])).astype(BF)
            al = mix(a, s)
            ar = mix(s, a)
            hup = dot(up[pl.ds(at, w), :], feat).astype(BF)
            h0, h1 = hup[:, : 2 * rem], hup[:, 2 * rem :]
            x = jnp.concatenate(
                [au[:, :full], ad[:, :full], al[:, :full], ar[:, :full], o[:, :full],
                 pair(au[:, full:], ad[:, full:]), pair(al[:, full:], ar[:, full:]),
                 pair(o[:, full:], h0), h1], axis=1)
            pre_n = dot(x, wt[...])
            xa = jnp.concatenate([pair(a[:, full:], h0), h1], axis=1)
            pre_a = dot(a[:, :full], wt[pl.ds(4 * full, full), :]) + dot(
                xa, wt[pl.ds(5 * full + 4 * rem, rem + zch), :])
            return jnp.concatenate([pre_a, pre_n], axis=0)

        def stage_hidden(pre):
            sg = 0.5 * jnp.tanh(0.5 * pre) + 0.5
            hidden = pre * sg
            return hidden.astype(BF), sg + hidden * (1.0 - sg)

        def stage_nll(t, par):
            at = t * w
            mu = par[:, :cp]
            sraw = par[:, cp:]
            e = jnp.exp(-jnp.abs(sraw))
            e1 = 1.0 + e
            sigma = 0.11 + (jnp.maximum(sraw, 0.0) + jnp.log(e1))
            inv = 1.0 / sigma
            y = jnp.concatenate([ae[pl.ds(half + at, w), :], nn[pl.ds(at, w), :]], axis=0).astype(F32)
            r = (y - mu) * inv
            nll = 0.5 * r * r + jnp.log(sigma)
            rsig = r * inv
            rs[pl.ds(2 * at, 2 * w), :] = rsig
            sgs = jnp.where(sraw >= 0.0, 1.0, e) / e1
            g_par = jnp.concatenate([-rsig, (1.0 - r * r) * inv * sgs], axis=1).astype(BF)
            return nll, g_par

        def stage_rate(t, nll):
            rate = jnp.sum(jnp.where(kidx < ch, nll, 0.0), axis=1, keepdims=True) * (1.0 / ch)
            spread = rate * cm[...].astype(F32)
            hi = spread.astype(BF)
            lo = (spread - hi.astype(F32)).astype(BF)
            rate_v[pl.ds(t * tr, tr), :] = dot(rg[...], hi) + dot(rg[...], lo)

        def stage_gp(t, g_hid, ds):
            at = t * w
            gp = (g_hid * ds).astype(BF)
            ga[pl.ds(at, w), :] = gp[:w]
            gne[pl.ds(half + at, w), :] = gp[w:]
            ut = upt[:, at : at + w]
            return dot(ut, gp[:w]) + dot(ut, gp[w:])

        every = range(tiles)
        pres, hids, pars, nlls, hback, gsums = [], [], [], [], [], []
        for t in every:
            pres.append(stage_pre(t))
        for t in every:
            hids.append(stage_hidden(pres[t]))
            pars.append(dot(hids[t][0], wo[...]))
        for t in every:
            nlls.append(stage_nll(t, pars[t]))
            hback.append(dot_t(nlls[t][1], wo[...]))
        for t in every:
            gsums.append(stage_gp(t, hback[t], hids[t][1]))
        gsum = sum(gsums[1:], gsums[0])

        csb[...] = dot(eb[...], gne[pl.ds(half, own), :]).astype(BF)
        start(gpre_c)

        hi = gsum.astype(BF)
        lo = (gsum - hi.astype(F32)).astype(BF)
        both = jnp.concatenate([hi, lo], axis=0)
        p0 = dot_t(both, wt[pl.ds(5 * ch + zch - 128, 128), :])
        p1 = dot_t(both, wt[pl.ds(5 * ch, zch - 128), :])
        g_h = jnp.concatenate([p0[:cells] + p0[cells:], p1[:cells] + p1[cells:]], axis=1)
        g_hz = (g_h * dz).astype(BF)
        gz[pl.ds(0, cells), :] = g_hz
        csz[...] = dot(ez[...], g_hz).astype(BF)
        start(gz_c)

        def main_w(d):
            return wt[pl.ds(d * full, full), :]

        def rest_w(d):
            return wt[pl.ds(5 * full + d * rem, rem), :]

        shifts, vns = [], []
        for t in every:
            at = t * w
            gn = gne[pl.ds(half + at, w), :]
            shifts.append(dot(sb[...], gn))
            nm = rs[pl.ds(2 * at + w, w), :full] + dot_t(gn, main_w(4))
            nq = rs[pl.ds(2 * at + w, w), full:ch] + dot_t(gn, rest_w(4))
            vns.append(jnp.concatenate([nm, nq], axis=1).astype(BF))
            gs = ga[pl.ds(at, w), :]
            m = rs[pl.ds(2 * at, w), :full] + dot_t(gs, main_w(4))
            q = rs[pl.ds(2 * at, w), full:ch] + dot_t(gs, rest_w(4))
            rs[pl.ds(2 * at, w), :full] = m
            rs[pl.ds(2 * at, w), full:ch] = q
            stage_rate(t, nlls[t][0])
        rate_copy = pltpu.make_async_copy(rate_v, rate_out, out_sem.at[0])
        rate_copy.start()

        wait_recv(gpre_c)
        outs = [rate_copy]
        for t in every:
            at = t * w
            gn = gne[pl.ds(half + at, w), :]
            gu = gne[pl.ds(at, w), :]
            gd = gne[pl.ds(2 * half + at, w), :]
            s = (shifts[t] + dot(qb[pl.ds(at, w), :], hcb[...])).astype(BF)
            gs = (gd, gu, mix(gn, s), mix(s, gn))
            m = rs[pl.ds(2 * at, w), :full]
            q = rs[pl.ds(2 * at, w), full:ch]
            for d in range(4):
                m = m + dot_t(gs[d], main_w(d))
                q = q + dot_t(gs[d], rest_w(d))
            va = jnp.concatenate([m, q], axis=1).astype(BF)
            vn = vns[t]
            for u in range(tr // 8):
                v = jnp.concatenate([va[u * n8 : (u + 1) * n8], vn[u * n8 : (u + 1) * n8]], axis=0)
                gl_v[pl.ds((t * tr + u * 8) * cols, 8 * cols), :] = dot(pt[...], v).astype(BF)
            span = pl.ds(t * tr * cols, tr * cols)
            c = pltpu.make_async_copy(gl_v.at[span], gl_out.at[span], out_sem.at[2 + t])
            c.start()
            outs.append(c)

        wait_recv(gz_c)
        taps = dot(tz[...], gz[...]).astype(BF)
        acc = jnp.zeros((cells, zch), F32)
        for ab in range(9):
            back = 8 - ab
            acc = acc + dot_t(taps[back * cells : (back + 1) * cells], hw[pl.ds(ab * zch, zch), :])
        gh_v[...] = acc
        c = pltpu.make_async_copy(gh_v, gh_out, out_sem.at[1])
        c.start()
        outs.append(c)
        for c in outs:
            c.wait()

        wait_send(hyper_c)
        wait_send(lat_c)
        wait_send(gpre_c)
        wait_send(gz_c)

    return kernel


def move(rate, gl, gh, rate_out, gl_out, gh_out, sem):
    parts = 4
    size = gl.shape[0] // parts
    copies = [pltpu.make_async_copy(rate, rate_out, sem.at[0]), pltpu.make_async_copy(gh, gh_out, sem.at[1])]
    for i in range(parts):
        span = pl.ds(i * size, size)
        copies.append(pltpu.make_async_copy(gl.at[span], gl_out.at[span], sem.at[2 + i]))
    for c in copies:
        c.start()
    for c in copies:
        c.wait()


def finish(*arrays):
    anyspec = pl.BlockSpec(memory_space=pl.ANY)
    return pl.pallas_call(
        move,
        out_shape=tuple(jax.ShapeDtypeStruct(a.shape, a.dtype) for a in arrays),
        in_specs=[anyspec] * 3,
        out_specs=(anyspec,) * 3,
        scratch_shapes=[pltpu.SemaphoreType.DMA((6,))],
    )(*arrays)


def solution(mesh):
    nrow, ncol = mesh.shape["row"], mesh.shape["col"]

    def local(latent, hyper, bounds, hyper_weight, prior_weight, ctx_weight, chan_weight, out_weight):
        rows, cols, ch = latent.shape
        zrows, zcols, zch = hyper.shape
        hid = prior_weight.shape[1]
        tr = 16
        half = cols // 2
        full = (ch // 256) * 256
        rem = ch - full
        cp = full + 2 * rem
        cells = zrows * zcols
        own = rows * half
        tabs = tables(rows, cols, zrows, zcols, tr)
        hr = rows // 2
        anyspec = pl.BlockSpec(memory_space=pl.ANY)
        v = lambda *s, dt=BF: pltpu.VMEM(s, dt)
        scratch = [
            v(rows * cols, ch), v(9 * zch, zch), v(5 * ch + zch, hid), v(hid, hid), v(hid, 2 * cp),
            *[v(*t.shape) for t in tabs],
            v(own + 2 * half, cp), v(own, cp), v(own, cp), v(2 * hr, cp), v(2 * hr, cp),
            v(cells + 128, zch), v(32, zch),
            v(own + 2 * half, hid), v(own, hid), v(rows * cols, cp, dt=F32), v(2 * hr, hid), v(2 * hr, hid),
            v(cells + 128, zch), v(32, zch),
            v(rows, cols, dt=F32), v(rows * cols, ch), v(cells, zch, dt=F32),
            pltpu.SemaphoreType.DMA((32,)), pltpu.SemaphoreType.DMA((2 + rows // tr,)), pltpu.SemaphoreType.DMA((24,)), pltpu.SemaphoreType.DMA((24,)),
        ]
        rate, gl, gh = pl.pallas_call(
            make_kernel(rows, cols, ch, zrows, zcols, zch, hid, tr, nrow, ncol),
            out_shape=(
                jax.ShapeDtypeStruct((rows, cols), F32),
                jax.ShapeDtypeStruct((rows * cols, ch), BF),
                jax.ShapeDtypeStruct((cells, zch), F32),
            ),
            in_specs=[pl.BlockSpec(memory_space=pltpu.SMEM)] + [anyspec] * (7 + len(tabs)),
            out_specs=(anyspec, anyspec, anyspec),
            scratch_shapes=scratch,
            compiler_params=pltpu.CompilerParams(
                collective_id=0, has_side_effects=True, vmem_limit_bytes=56 * 1024 * 1024),
        )(
            bounds, latent.reshape(rows * cols, ch), hyper.reshape(cells, zch),
            hyper_weight.reshape(9 * zch, zch), prior_weight, ctx_weight.reshape(4 * ch, hid),
            chan_weight, out_weight, *[jnp.asarray(t) for t in tabs],
        )
        rate, gl, gh = finish(rate, gl, gh)
        return rate, gl.reshape(rows, cols, ch), gh.reshape(zrows, zcols, zch)

    in_specs = (
        P(("parts", "row"), "col", None),
        P(("parts", "row"), "col", None),
        P(),
        P(),
        P(),
        P(),
        P(),
        P(),
    )
    out_specs = (
        P(("parts", "row"), "col"),
        P(("parts", "row"), "col", None),
        P(("parts", "row"), "col", None),
    )
    return jax.shard_map(local, mesh=mesh, in_specs=in_specs, out_specs=out_specs, check_vma=False)
```

```python
import jax
import jax.numpy as jnp
import numpy as np
from jax import lax
from jax.experimental import pallas as pl
from jax.experimental.pallas import tpu as pltpu
from jax.sharding import PartitionSpec as P

BF = jnp.bfloat16
F32 = jnp.float32
DIRS = ((-1, 0), (1, 0), (0, -1), (0, 1), (-1, -1), (-1, 1), (1, -1), (1, 1))
OPP = (1, 0, 3, 2, 7, 6, 5, 4)


def dot(a, b):
    return jnp.dot(a, b, preferred_element_type=F32)


def dot_t(a, b):
    return lax.dot_general(a, b, (((1,), (1,)), ((), ())), preferred_element_type=F32)


def tables(rows, cols, zrows, zcols, tr):
    half = cols // 2
    sub = 8
    m = np.arange(sub * half)
    ir, k = m // half, m % half
    ps = np.zeros((3 * sub * half, sub * cols), np.float32)
    n = sub * half
    ps[m, ir * cols + 2 * k + ir % 2] = 1
    ps[n + m, ir * cols + 2 * k + 1 - ir % 2] = 1
    for q in m:
        kk = k[q] + (1 if ir[q] % 2 == 0 else -1)
        if 0 <= kk < half:
            ps[2 * n + q, ir[q] * cols + 2 * kk + ir[q] % 2] = 1
    pt = ps[: 2 * n].T.copy()
    m = np.arange(tr * half)
    ir, k = m // half, m % half
    sb = np.zeros((tr * half, tr * half), np.float32)
    for q in m:
        kk = k[q] + (-1 if ir[q] % 2 == 0 else 1)
        if 0 <= kk < half:
            sb[q, ir[q] * half + kk] = 1
    m = np.arange(rows * half)
    i, k = m // half, m % half
    up = np.zeros((rows * half, zrows * zcols), np.float32)
    up[m, (i // 4) * zcols + k // 2] = 1
    qf = np.zeros((rows * half, rows), np.float32)
    qb = np.zeros((rows * half, rows), np.float32)
    ef = np.zeros((rows, rows * half), np.float32)
    eb = np.zeros((rows, rows * half), np.float32)
    for r in range(rows):
        e = r // 2 + (rows // 2 if r % 2 else 0)
        qf[r * half + (half - 1 if r % 2 == 0 else 0), e] = 1
        qb[r * half + (0 if r % 2 == 0 else half - 1), e] = 1
        ef[e, r * half + (0 if r % 2 == 0 else half - 1)] = 1
        eb[e, r * half + (half - 1 if r % 2 == 0 else 0)] = 1
    cells = zrows * zcols
    tz = np.zeros((9 * cells, cells + 8 * 16), np.float32)
    for a in range(3):
        for b in range(3):
            for zi in range(zrows):
                for zj in range(zcols):
                    y, x = zi + a - 1, zj + b - 1
                    dr = -1 if y < 0 else (1 if y >= zrows else 0)
                    dc = -1 if x < 0 else (1 if x >= zcols else 0)
                    if (dr, dc) == (0, 0):
                        s = y * zcols + x
                    else:
                        s = cells + 16 * DIRS.index((dr, dc))
                        if dr == 0:
                            s += y
                        else:
                            s += (16 - zcols if dr < 0 else 0) + x % zcols
                    tz[(a * 3 + b) * cells + zi * zcols + zj, s] = 1
    ez = np.zeros((32, cells), np.float32)
    for zi in range(zrows):
        ez[zi, zi * zcols] = 1
        ez[16 + zi, zi * zcols + zcols - 1] = 1
    m = np.arange(tr * half)
    ir, k = m // half, m % half
    w = tr * half
    rg = np.zeros((tr, 2 * w), np.float32)
    rg[ir, m] = 1
    rg[ir, w + m] = 1
    cm = np.zeros((2 * w, cols), np.float32)
    cm[m, 2 * k + ir % 2] = 1
    cm[w + m, 2 * k + 1 - ir % 2] = 1
    return [x.astype(jnp.bfloat16) for x in (ps, pt, sb, up, up.T.copy(), qf, qb, ef, eb, tz, ez, rg, cm)]


def make_kernel(rows, cols, ch, zrows, zcols, zch, hid, tr, nrow, ncol):
    half = cols // 2
    full = (ch // 256) * 256
    rem = ch - full
    cp = full + 2 * rem
    cells = zrows * zcols
    w = tr * half
    tiles = rows // tr
    own = rows * half

    def kernel(*refs):
        (bounds, latent, hyper, hw_in, pw_in, cw_in, kw_in, ow_in, *tabs) = refs[:21]
        rate_out, gl_out, gh_out = refs[21:24]
        (lat, hw, wt, owr, wo, ps, pt, sb, up, upt, qf, qb, ef, eb, tz, ez, rg, cm,
         ae, nn, ss, hcf, csf, he, csh, gne, ga, rs, hcb, csb, gz, csz, rate_v, gl_v, gh_v,
         in_sem, out_sem, send_sem, recv_sem) = refs[24:]
        tab_v = (ps, pt, sb, up, upt, qf, qb, ef, eb, tz, ez, rg, cm)
        my_r = lax.axis_index("row")
        my_c = lax.axis_index("col")

        def there(d):
            dr, dc = DIRS[d]
            ok = my_r >= 0
            if dr < 0:
                ok = my_r > 0
            if dr > 0:
                ok = my_r < nrow - 1
            if dc < 0:
                ok = ok & (my_c > 0)
            if dc > 0:
                ok = ok & (my_c < ncol - 1)
            return ok

        def dev(d):
            return {"row": my_r + DIRS[d][0], "col": my_c + DIRS[d][1]}

        barrier = pltpu.get_barrier_semaphore()
        for d in range(8):
            @pl.when(there(d))
            def _(d=d):
                pl.semaphore_signal(barrier, inc=1, device_id=dev(d), device_id_type=pl.DeviceIdType.MESH)

        loads = []

        def load(src, dst):
            c = pltpu.make_async_copy(src, dst, in_sem.at[len(loads)])
            c.start()
            loads.append(c)
            return len(loads) - 1

        ld_lat = load(latent, lat)
        ld_hyper = load(hyper, he.at[pl.ds(0, cells)])
        early = (0, 7, 10)
        ld_early = [load(tabs[i], tab_v[i]) for i in early]
        ld_w = []
        for d in range(4):
            ld_w.append(load(cw_in.at[pl.ds(d * ch, full)], wt.at[pl.ds(d * full, full)]))
            ld_w.append(load(cw_in.at[pl.ds(d * ch + full, rem)], wt.at[pl.ds(5 * full + d * rem, rem)]))
        ld_w.append(load(kw_in.at[pl.ds(0, full)], wt.at[pl.ds(4 * full, full)]))
        ld_w.append(load(kw_in.at[pl.ds(full, rem)], wt.at[pl.ds(5 * full + 4 * rem, rem)]))
        ld_w.append(load(pw_in.at[pl.ds(128, zch - 128)], wt.at[pl.ds(5 * ch, zch - 128)]))
        ld_w.append(load(pw_in.at[pl.ds(0, 128)], wt.at[pl.ds(5 * ch + zch - 128, 128)]))
        ld_ow = load(ow_in, owr)
        ld_hw = load(hw_in, hw)
        ld_late = [load(tabs[i], tab_v[i]) for i in range(len(tabs)) if i not in early]

        def absent(d, fill):
            @pl.when(jnp.logical_not(there(d)))
            def _():
                fill()

        def zero(ref, start, size):
            def fill():
                ref[pl.ds(start, size), :] = jnp.zeros((size, ref.shape[1]), ref.dtype)
            return fill

        for d in range(8):
            absent(d, zero(he, cells + 16 * d, 16))
            absent(d, zero(gz, cells + 16 * d, 16))
        absent(0, zero(ae, 0, half))
        absent(1, zero(ae, half + own, half))
        absent(0, zero(gne, 0, half))
        absent(1, zero(gne, half + own, half))
        hr = rows // 2
        absent(3, zero(hcf, 0, hr))
        absent(2, zero(hcf, hr, hr))
        absent(2, zero(hcb, 0, hr))
        absent(3, zero(hcb, hr, hr))

        def remote(idx, d, src, dst):
            return pltpu.make_async_remote_copy(
                src_ref=src, dst_ref=dst, send_sem=send_sem.at[idx], recv_sem=recv_sem.at[idx],
                device_id=dev(d), device_id_type=pl.DeviceIdType.MESH)

        def hyper_copies(base, ext, col):
            out = []
            for d, (dr, dc) in enumerate(DIRS):
                if dr < 0:
                    src = ext.at[pl.ds(0, 16)]
                elif dr > 0:
                    src = ext.at[pl.ds(cells - 16, 16)]
                else:
                    src = col.at[pl.ds(0 if dc < 0 else 16, 16)]
                out.append((d, OPP[d], remote(base + OPP[d], d, src, ext.at[pl.ds(cells + 16 * OPP[d], 16)])))
            return out

        def side_copies(base, ext, col, halo, left_first):
            lf = 0 if left_first else hr
            rf = hr - lf
            return [
                (0, 1, remote(base + 1, 0, ext.at[pl.ds(half, half)], ext.at[pl.ds(half + own, half)])),
                (1, 0, remote(base + 0, 1, ext.at[pl.ds(own, half)], ext.at[pl.ds(0, half)])),
                (2, 3, remote(base + 3, 2, col.at[pl.ds(lf, hr)], halo.at[pl.ds(lf, hr)])),
                (3, 2, remote(base + 2, 3, col.at[pl.ds(rf, hr)], halo.at[pl.ds(rf, hr)])),
            ]

        hyper_c = hyper_copies(0, he, csh)
        lat_c = side_copies(8, ae, csf, hcf, True)
        gpre_c = side_copies(12, gne, csb, hcb, False)
        gz_c = hyper_copies(16, gz, csz)

        def start(copies):
            for d, _, c in copies:
                @pl.when(there(d))
                def _(c=c):
                    c.start()

        def wait_recv(copies):
            for _, o, c in copies:
                @pl.when(there(o))
                def _(c=c):
                    c.wait_recv()

        def wait_send(copies):
            for d, _, c in copies:
                @pl.when(there(d))
                def _(c=c):
                    c.wait_send()

        loads[ld_lat].wait()
        loads[ld_hyper].wait()
        for i in ld_early:
            loads[i].wait()
        csh[...] = dot(ez[...], he[pl.ds(0, cells), :]).astype(BF)
        n8 = 8 * half
        for t in range(rows // 8):
            y = dot(ps[...], lat[pl.ds(t * 8 * cols, 8 * cols), :])
            y = jnp.concatenate([y[:, :full], y[:, full:], y[:, full:]], axis=1).astype(BF)
            ae[pl.ds(half + t * n8, n8), :] = y[:n8]
            nn[pl.ds(t * n8, n8), :] = y[n8 : 2 * n8]
            ss[pl.ds(t * n8, n8), :] = y[2 * n8 :]
        csf[...] = dot(ef[...], ae[pl.ds(half, own), :]).astype(BF)

        count = jnp.int32(0)
        for d in range(8):
            count = count + there(d).astype(jnp.int32)
        pl.semaphore_wait(barrier, count)
        start(hyper_c)
        start(lat_c)

        def ids(shape, dim, period, width):
            c = lax.broadcasted_iota(jnp.int32, shape, dim)
            c = jnp.where(c >= period, c - period, c)
            s = jnp.zeros(shape, jnp.int32)
            for g in range(1, 5):
                s = s + (c >= bounds[g]).astype(jnp.int32)
            return jnp.where(c < width, s, -1)

        col_id = ids((1, hid), 1, ch, ch)
        row_id = ids((ch, 1), 0, ch, ch)
        same = jnp.where(row_id == col_id, 1.0, 0.0).astype(BF)
        prev = jnp.where(row_id < col_id, 1.0, 0.0).astype(BF)
        for i in ld_w:
            loads[i].wait()
        for d in range(5):
            mask = prev if d == 4 else same
            a = pl.ds(d * full, full)
            wt[a, :] = wt[a, :] * mask[:full]
            b = pl.ds(5 * full + d * rem, rem)
            wt[b, :] = wt[b, :] * mask[full:]
        hid_id = ids((hid, 1), 0, ch, ch)
        par_id = ids((1, 2 * cp), 1, cp, ch)
        omask = jnp.where(hid_id == par_id, 1.0, 0.0).astype(BF)
        loads[ld_ow].wait()
        raw = owr[...].astype(F32)
        pad = jnp.zeros((hid, cp - ch), F32)
        wide = jnp.concatenate([raw[:, :ch], pad, raw[:, ch:], pad], axis=1).astype(BF)
        wo[...] = wide * omask

        loads[ld_hw].wait()
        for i in ld_late:
            loads[i].wait()
        wait_recv(hyper_c)
        taps = dot(tz[...], he[...]).astype(BF)
        hz = jnp.zeros((cells, zch), F32)
        for ab in range(9):
            hz = hz + dot(taps[ab * cells : (ab + 1) * cells], hw[pl.ds(ab * zch, zch), :])
        sz = jax.nn.sigmoid(hz)
        dz = sz * (1.0 + hz * (1.0 - sz))
        f = hz * sz
        feat = jnp.concatenate([jnp.zeros((cells, rem), F32), f[:, 128:], f[:, :128]], axis=1).astype(BF)
        wait_recv(lat_c)

        def mix(even, odd):
            return jnp.concatenate(
                [(even if i % 2 == 0 else odd)[i * half : (i + 1) * half] for i in range(tr)], axis=0)

        lane = lax.broadcasted_iota(jnp.int32, (w, 2 * rem), 1)
        left = lane < rem

        def pair(a, b):
            return jnp.where(left, a, b)

        kidx = lax.broadcasted_iota(jnp.int32, (2 * w, cp), 1)

        def stage_pre(t):
            at = t * w
            a = ae[pl.ds(half + at, w), :]
            au = ae[pl.ds(at, w), :]
            ad = ae[pl.ds(2 * half + at, w), :]
            o = nn[pl.ds(at, w), :]
            s = (ss[pl.ds(at, w), :].astype(F32) + dot(qf[pl.ds(at, w), :], hcf[...])).astype(BF)
            al = mix(a, s)
            ar = mix(s, a)
            hup = dot(up[pl.ds(at, w), :], feat).astype(BF)
            h0, h1 = hup[:, : 2 * rem], hup[:, 2 * rem :]
            x = jnp.concatenate(
                [au[:, :full], ad[:, :full], al[:, :full], ar[:, :full], o[:, :full],
                 pair(au[:, full:], ad[:, full:]), pair(al[:, full:], ar[:, full:]),
                 pair(o[:, full:], h0), h1], axis=1)
            pre_n = dot(x, wt[...])
            xa = jnp.concatenate([pair(a[:, full:], h0), h1], axis=1)
            pre_a = dot(a[:, :full], wt[pl.ds(4 * full, full), :]) + dot(
                xa, wt[pl.ds(5 * full + 4 * rem, rem + zch), :])
            return jnp.concatenate([pre_a, pre_n], axis=0)

        def stage_hidden(pre):
            sg = 0.5 * jnp.tanh(0.5 * pre) + 0.5
            hidden = pre * sg
            return hidden.astype(BF), sg + hidden * (1.0 - sg)

        def stage_nll(t, par):
            at = t * w
            mu = par[:, :cp]
            sraw = par[:, cp:]
            e = jnp.exp(-jnp.abs(sraw))
            e1 = 1.0 + e
            sigma = 0.11 + (jnp.maximum(sraw, 0.0) + jnp.log(e1))
            inv = 1.0 / sigma
            y = jnp.concatenate([ae[pl.ds(half + at, w), :], nn[pl.ds(at, w), :]], axis=0).astype(F32)
            r = (y - mu) * inv
            nll = 0.5 * r * r + jnp.log(sigma)
            rsig = r * inv
            rs[pl.ds(2 * at, 2 * w), :] = rsig
            sgs = jnp.where(sraw >= 0.0, 1.0, e) / e1
            g_par = jnp.concatenate([-rsig, (1.0 - r * r) * inv * sgs], axis=1).astype(BF)
            return nll, g_par

        def stage_rate(t, nll):
            rate = jnp.sum(jnp.where(kidx < ch, nll, 0.0), axis=1, keepdims=True) * (1.0 / ch)
            spread = rate * cm[...].astype(F32)
            hi = spread.astype(BF)
            lo = (spread - hi.astype(F32)).astype(BF)
            rate_v[pl.ds(t * tr, tr), :] = dot(rg[...], hi) + dot(rg[...], lo)

        def stage_gp(t, g_hid, ds):
            at = t * w
            gp = (g_hid * ds).astype(BF)
            ga[pl.ds(at, w), :] = gp[:w]
            gne[pl.ds(half + at, w), :] = gp[w:]
            ut = upt[:, at : at + w]
            return dot(ut, gp[:w]) + dot(ut, gp[w:])

        every = range(tiles)
        pres, hids, pars, nlls, hback, gsums = [], [], [], [], [], []
        for t in every:
            pres.append(stage_pre(t))
        for t in every:
            hids.append(stage_hidden(pres[t]))
            pars.append(dot(hids[t][0], wo[...]))
        for t in every:
            nlls.append(stage_nll(t, pars[t]))
            hback.append(dot_t(nlls[t][1], wo[...]))
        for t in every:
            gsums.append(stage_gp(t, hback[t], hids[t][1]))
        gsum = sum(gsums[1:], gsums[0])

        csb[...] = dot(eb[...], gne[pl.ds(half, own), :]).astype(BF)
        start(gpre_c)

        hi = gsum.astype(BF)
        lo = (gsum - hi.astype(F32)).astype(BF)
        both = jnp.concatenate([hi, lo], axis=0)
        p0 = dot_t(both, wt[pl.ds(5 * ch + zch - 128, 128), :])
        p1 = dot_t(both, wt[pl.ds(5 * ch, zch - 128), :])
        g_h = jnp.concatenate([p0[:cells] + p0[cells:], p1[:cells] + p1[cells:]], axis=1)
        g_hz = (g_h * dz).astype(BF)
        gz[pl.ds(0, cells), :] = g_hz
        csz[...] = dot(ez[...], g_hz).astype(BF)
        start(gz_c)

        def main_w(d):
            return wt[pl.ds(d * full, full), :]

        def rest_w(d):
            return wt[pl.ds(5 * full + d * rem, rem), :]

        shifts, vns = [], []
        for t in every:
            at = t * w
            gn = gne[pl.ds(half + at, w), :]
            shifts.append(dot(sb[...], gn))
            nm = rs[pl.ds(2 * at + w, w), :full] + dot_t(gn, main_w(4))
            nq = rs[pl.ds(2 * at + w, w), full:ch] + dot_t(gn, rest_w(4))
            vns.append(jnp.concatenate([nm, nq], axis=1).astype(BF))
            gs = ga[pl.ds(at, w), :]
            m = rs[pl.ds(2 * at, w), :full] + dot_t(gs, main_w(4))
            q = rs[pl.ds(2 * at, w), full:ch] + dot_t(gs, rest_w(4))
            rs[pl.ds(2 * at, w), :full] = m
            rs[pl.ds(2 * at, w), full:ch] = q
            stage_rate(t, nlls[t][0])
        rate_copy = pltpu.make_async_copy(rate_v, rate_out, out_sem.at[0])
        rate_copy.start()

        wait_recv(gpre_c)
        outs = [rate_copy]
        for t in every:
            at = t * w
            gn = gne[pl.ds(half + at, w), :]
            gu = gne[pl.ds(at, w), :]
            gd = gne[pl.ds(2 * half + at, w), :]
            s = (shifts[t] + dot(qb[pl.ds(at, w), :], hcb[...])).astype(BF)
            gs = (gd, gu, mix(gn, s), mix(s, gn))
            m = rs[pl.ds(2 * at, w), :full]
            q = rs[pl.ds(2 * at, w), full:ch]
            for d in range(4):
                m = m + dot_t(gs[d], main_w(d))
                q = q + dot_t(gs[d], rest_w(d))
            va = jnp.concatenate([m, q], axis=1).astype(BF)
            vn = vns[t]
            for u in range(tr // 8):
                v = jnp.concatenate([va[u * n8 : (u + 1) * n8], vn[u * n8 : (u + 1) * n8]], axis=0)
                gl_v[pl.ds((t * tr + u * 8) * cols, 8 * cols), :] = dot(pt[...], v).astype(BF)
            span = pl.ds(t * tr * cols, tr * cols)
            c = pltpu.make_async_copy(gl_v.at[span], gl_out.at[span], out_sem.at[2 + t])
            c.start()
            outs.append(c)

        wait_recv(gz_c)
        taps = dot(tz[...], gz[...]).astype(BF)
        acc = jnp.zeros((cells, zch), F32)
        for ab in range(9):
            back = 8 - ab
            acc = acc + dot_t(taps[back * cells : (back + 1) * cells], hw[pl.ds(ab * zch, zch), :])
        gh_v[...] = acc
        c = pltpu.make_async_copy(gh_v, gh_out, out_sem.at[1])
        c.start()
        outs.append(c)
        for c in outs:
            c.wait()

        wait_send(hyper_c)
        wait_send(lat_c)
        wait_send(gpre_c)
        wait_send(gz_c)

    return kernel


def move(rate, gl, gh, rate_out, gl_out, gh_out, rate_v, gl_v, gh_v, sem, sem_out):
    parts = 4
    size = gl.shape[0] // parts
    triples = [(rate, rate_v, rate_out), (gh, gh_v, gh_out)]
    for i in range(parts):
        span = pl.ds(i * size, size)
        triples.append((gl.at[span], gl_v.at[span], gl_out.at[span]))
    ins = [pltpu.make_async_copy(a, b, sem.at[i]) for i, (a, b, _) in enumerate(triples)]
    outs = [pltpu.make_async_copy(b, c, sem_out.at[i]) for i, (_, b, c) in enumerate(triples)]
    for c in ins:
        c.start()
    for a, b in zip(ins, outs):
        a.wait()
        b.start()
    for c in outs:
        c.wait()


def finish(*arrays):
    anyspec = pl.BlockSpec(memory_space=pl.ANY)
    return pl.pallas_call(
        move,
        out_shape=tuple(jax.ShapeDtypeStruct(a.shape, a.dtype) for a in arrays),
        in_specs=[anyspec] * 3,
        out_specs=(anyspec,) * 3,
        scratch_shapes=[pltpu.VMEM(a.shape, a.dtype) for a in arrays] + [pltpu.SemaphoreType.DMA((6,))] * 2,
    )(*arrays)


def solution(mesh):
    nrow, ncol = mesh.shape["row"], mesh.shape["col"]

    def local(latent, hyper, bounds, hyper_weight, prior_weight, ctx_weight, chan_weight, out_weight):
        rows, cols, ch = latent.shape
        zrows, zcols, zch = hyper.shape
        hid = prior_weight.shape[1]
        tr = 16
        half = cols // 2
        full = (ch // 256) * 256
        rem = ch - full
        cp = full + 2 * rem
        cells = zrows * zcols
        own = rows * half
        tabs = tables(rows, cols, zrows, zcols, tr)
        hr = rows // 2
        anyspec = pl.BlockSpec(memory_space=pl.ANY)
        v = lambda *s, dt=BF: pltpu.VMEM(s, dt)
        scratch = [
            v(rows * cols, ch), v(9 * zch, zch), v(5 * ch + zch, hid), v(hid, hid), v(hid, 2 * cp),
            *[v(*t.shape) for t in tabs],
            v(own + 2 * half, cp), v(own, cp), v(own, cp), v(2 * hr, cp), v(2 * hr, cp),
            v(cells + 128, zch), v(32, zch),
            v(own + 2 * half, hid), v(own, hid), v(rows * cols, cp, dt=F32), v(2 * hr, hid), v(2 * hr, hid),
            v(cells + 128, zch), v(32, zch),
            v(rows, cols, dt=F32), v(rows * cols, ch), v(cells, zch, dt=F32),
            pltpu.SemaphoreType.DMA((32,)), pltpu.SemaphoreType.DMA((2 + rows // tr,)), pltpu.SemaphoreType.DMA((24,)), pltpu.SemaphoreType.DMA((24,)),
        ]
        rate, gl, gh = pl.pallas_call(
            make_kernel(rows, cols, ch, zrows, zcols, zch, hid, tr, nrow, ncol),
            out_shape=(
                jax.ShapeDtypeStruct((rows, cols), F32),
                jax.ShapeDtypeStruct((rows * cols, ch), BF),
                jax.ShapeDtypeStruct((cells, zch), F32),
            ),
            in_specs=[pl.BlockSpec(memory_space=pltpu.SMEM)] + [anyspec] * (7 + len(tabs)),
            out_specs=(anyspec, anyspec, anyspec),
            scratch_shapes=scratch,
            compiler_params=pltpu.CompilerParams(
                collective_id=0, has_side_effects=True, vmem_limit_bytes=56 * 1024 * 1024),
        )(
            bounds, latent.reshape(rows * cols, ch), hyper.reshape(cells, zch),
            hyper_weight.reshape(9 * zch, zch), prior_weight, ctx_weight.reshape(4 * ch, hid),
            chan_weight, out_weight, *[jnp.asarray(t) for t in tabs],
        )
        rate, gl, gh = finish(rate, gl, gh)
        return rate, gl.reshape(rows, cols, ch), gh.reshape(zrows, zcols, zch)

    in_specs = (
        P(("parts", "row"), "col", None),
        P(("parts", "row"), "col", None),
        P(),
        P(),
        P(),
        P(),
        P(),
        P(),
    )
    out_specs = (
        P(("parts", "row"), "col"),
        P(("parts", "row"), "col", None),
        P(("parts", "row"), "col", None),
    )
    return jax.shard_map(local, mesh=mesh, in_specs=in_specs, out_specs=out_specs, check_vma=False)
```

```python
import jax
import jax.numpy as jnp
import numpy as np
from jax import lax
from jax.experimental import pallas as pl
from jax.experimental.pallas import tpu as pltpu
from jax.sharding import PartitionSpec as P

BF = jnp.bfloat16
F32 = jnp.float32
DIRS = ((-1, 0), (1, 0), (0, -1), (0, 1), (-1, -1), (-1, 1), (1, -1), (1, 1))
OPP = (1, 0, 3, 2, 7, 6, 5, 4)


def dot(a, b):
    return jnp.dot(a, b, preferred_element_type=F32)


def dot_t(a, b):
    return lax.dot_general(a, b, (((1,), (1,)), ((), ())), preferred_element_type=F32)


def tables(rows, cols, zrows, zcols, tr):
    half = cols // 2
    sub = 8
    m = np.arange(sub * half)
    ir, k = m // half, m % half
    ps = np.zeros((3 * sub * half, sub * cols), np.float32)
    n = sub * half
    ps[m, ir * cols + 2 * k + ir % 2] = 1
    ps[n + m, ir * cols + 2 * k + 1 - ir % 2] = 1
    for q in m:
        kk = k[q] + (1 if ir[q] % 2 == 0 else -1)
        if 0 <= kk < half:
            ps[2 * n + q, ir[q] * cols + 2 * kk + ir[q] % 2] = 1
    pt = ps[: 2 * n].T.copy()
    m = np.arange(tr * half)
    ir, k = m // half, m % half
    sb = np.zeros((tr * half, tr * half), np.float32)
    for q in m:
        kk = k[q] + (-1 if ir[q] % 2 == 0 else 1)
        if 0 <= kk < half:
            sb[q, ir[q] * half + kk] = 1
    m = np.arange(rows * half)
    i, k = m // half, m % half
    up = np.zeros((rows * half, zrows * zcols), np.float32)
    up[m, (i // 4) * zcols + k // 2] = 1
    qf = np.zeros((rows * half, rows), np.float32)
    qb = np.zeros((rows * half, rows), np.float32)
    ef = np.zeros((rows, rows * half), np.float32)
    eb = np.zeros((rows, rows * half), np.float32)
    for r in range(rows):
        e = r // 2 + (rows // 2 if r % 2 else 0)
        qf[r * half + (half - 1 if r % 2 == 0 else 0), e] = 1
        qb[r * half + (0 if r % 2 == 0 else half - 1), e] = 1
        ef[e, r * half + (0 if r % 2 == 0 else half - 1)] = 1
        eb[e, r * half + (half - 1 if r % 2 == 0 else 0)] = 1
    cells = zrows * zcols
    tz = np.zeros((9 * cells, cells + 8 * 16), np.float32)
    for a in range(3):
        for b in range(3):
            for zi in range(zrows):
                for zj in range(zcols):
                    y, x = zi + a - 1, zj + b - 1
                    dr = -1 if y < 0 else (1 if y >= zrows else 0)
                    dc = -1 if x < 0 else (1 if x >= zcols else 0)
                    if (dr, dc) == (0, 0):
                        s = y * zcols + x
                    else:
                        s = cells + 16 * DIRS.index((dr, dc))
                        if dr == 0:
                            s += y
                        else:
                            s += (16 - zcols if dr < 0 else 0) + x % zcols
                    tz[(a * 3 + b) * cells + zi * zcols + zj, s] = 1
    ez = np.zeros((32, cells), np.float32)
    for zi in range(zrows):
        ez[zi, zi * zcols] = 1
        ez[16 + zi, zi * zcols + zcols - 1] = 1
    m = np.arange(tr * half)
    ir, k = m // half, m % half
    w = tr * half
    rg = np.zeros((tr, 2 * w), np.float32)
    rg[ir, m] = 1
    rg[ir, w + m] = 1
    cm = np.zeros((2 * w, cols), np.float32)
    cm[m, 2 * k + ir % 2] = 1
    cm[w + m, 2 * k + 1 - ir % 2] = 1
    return [x.astype(jnp.bfloat16) for x in (ps, pt, sb, up, up.T.copy(), qf, qb, ef, eb, tz, ez, rg, cm)]


def make_kernel(rows, cols, ch, zrows, zcols, zch, hid, tr, nrow, ncol):
    half = cols // 2
    full = (ch // 256) * 256
    rem = ch - full
    cp = full + 2 * rem
    cells = zrows * zcols
    w = tr * half
    tiles = rows // tr
    own = rows * half

    def kernel(*refs):
        (bounds, latent, hyper, hw_in, pw_in, cw_in, kw_in, ow_in, *tabs) = refs[:21]
        rate_out, gl_out, gh_out = refs[21:24]
        (lat, hw, wt, owr, wo, ps, pt, sb, up, upt, qf, qb, ef, eb, tz, ez, rg, cm,
         ae, nn, ss, hcf, csf, he, csh, gne, ga, rs, hcb, csb, gz, csz, rate_v, gl_v, gh_v,
         in_sem, out_sem, send_sem, recv_sem) = refs[24:]
        tab_v = (ps, pt, sb, up, upt, qf, qb, ef, eb, tz, ez, rg, cm)
        my_r = lax.axis_index("row")
        my_c = lax.axis_index("col")

        def there(d):
            dr, dc = DIRS[d]
            ok = my_r >= 0
            if dr < 0:
                ok = my_r > 0
            if dr > 0:
                ok = my_r < nrow - 1
            if dc < 0:
                ok = ok & (my_c > 0)
            if dc > 0:
                ok = ok & (my_c < ncol - 1)
            return ok

        def dev(d):
            return {"row": my_r + DIRS[d][0], "col": my_c + DIRS[d][1]}

        barrier = pltpu.get_barrier_semaphore()
        for d in range(8):
            @pl.when(there(d))
            def _(d=d):
                pl.semaphore_signal(barrier, inc=1, device_id=dev(d), device_id_type=pl.DeviceIdType.MESH)

        loads = []

        def load(src, dst):
            c = pltpu.make_async_copy(src, dst, in_sem.at[len(loads)])
            c.start()
            loads.append(c)
            return len(loads) - 1

        ld_lat = load(latent, lat)
        ld_hyper = load(hyper, he.at[pl.ds(0, cells)])
        early = (0, 7, 10)
        ld_early = [load(tabs[i], tab_v[i]) for i in early]
        ld_w = []
        for d in range(4):
            ld_w.append(load(cw_in.at[pl.ds(d * ch, full)], wt.at[pl.ds(d * full, full)]))
            ld_w.append(load(cw_in.at[pl.ds(d * ch + full, rem)], wt.at[pl.ds(5 * full + d * rem, rem)]))
        ld_w.append(load(kw_in.at[pl.ds(0, full)], wt.at[pl.ds(4 * full, full)]))
        ld_w.append(load(kw_in.at[pl.ds(full, rem)], wt.at[pl.ds(5 * full + 4 * rem, rem)]))
        ld_w.append(load(pw_in.at[pl.ds(128, zch - 128)], wt.at[pl.ds(5 * ch, zch - 128)]))
        ld_w.append(load(pw_in.at[pl.ds(0, 128)], wt.at[pl.ds(5 * ch + zch - 128, 128)]))
        ld_ow = load(ow_in, owr)
        ld_hw = load(hw_in, hw)
        ld_late = [load(tabs[i], tab_v[i]) for i in range(len(tabs)) if i not in early]

        def absent(d, fill):
            @pl.when(jnp.logical_not(there(d)))
            def _():
                fill()

        def zero(ref, start, size):
            def fill():
                ref[pl.ds(start, size), :] = jnp.zeros((size, ref.shape[1]), ref.dtype)
            return fill

        for d in range(8):
            absent(d, zero(he, cells + 16 * d, 16))
            absent(d, zero(gz, cells + 16 * d, 16))
        absent(0, zero(ae, 0, half))
        absent(1, zero(ae, half + own, half))
        absent(0, zero(gne, 0, half))
        absent(1, zero(gne, half + own, half))
        hr = rows // 2
        absent(3, zero(hcf, 0, hr))
        absent(2, zero(hcf, hr, hr))
        absent(2, zero(hcb, 0, hr))
        absent(3, zero(hcb, hr, hr))

        def remote(idx, d, src, dst):
            return pltpu.make_async_remote_copy(
                src_ref=src, dst_ref=dst, send_sem=send_sem.at[idx], recv_sem=recv_sem.at[idx],
                device_id=dev(d), device_id_type=pl.DeviceIdType.MESH)

        def hyper_copies(base, ext, col):
            out = []
            for d, (dr, dc) in enumerate(DIRS):
                if dr < 0:
                    src = ext.at[pl.ds(0, 16)]
                elif dr > 0:
                    src = ext.at[pl.ds(cells - 16, 16)]
                else:
                    src = col.at[pl.ds(0 if dc < 0 else 16, 16)]
                out.append((d, OPP[d], remote(base + OPP[d], d, src, ext.at[pl.ds(cells + 16 * OPP[d], 16)])))
            return out

        def side_copies(base, ext, col, halo, left_first):
            lf = 0 if left_first else hr
            rf = hr - lf
            return [
                (0, 1, remote(base + 1, 0, ext.at[pl.ds(half, half)], ext.at[pl.ds(half + own, half)])),
                (1, 0, remote(base + 0, 1, ext.at[pl.ds(own, half)], ext.at[pl.ds(0, half)])),
                (2, 3, remote(base + 3, 2, col.at[pl.ds(lf, hr)], halo.at[pl.ds(lf, hr)])),
                (3, 2, remote(base + 2, 3, col.at[pl.ds(rf, hr)], halo.at[pl.ds(rf, hr)])),
            ]

        hyper_c = hyper_copies(0, he, csh)
        lat_c = side_copies(8, ae, csf, hcf, True)
        gpre_c = side_copies(12, gne, csb, hcb, False)
        gz_c = hyper_copies(16, gz, csz)

        def start(copies):
            for d, _, c in copies:
                @pl.when(there(d))
                def _(c=c):
                    c.start()

        def wait_recv(copies):
            for _, o, c in copies:
                @pl.when(there(o))
                def _(c=c):
                    c.wait_recv()

        def wait_send(copies):
            for d, _, c in copies:
                @pl.when(there(d))
                def _(c=c):
                    c.wait_send()

        loads[ld_lat].wait()
        loads[ld_hyper].wait()
        for i in ld_early:
            loads[i].wait()
        csh[...] = dot(ez[...], he[pl.ds(0, cells), :]).astype(BF)
        count = jnp.int32(0)
        for d in range(8):
            count = count + there(d).astype(jnp.int32)
        pl.semaphore_wait(barrier, count)
        start(hyper_c)
        n8 = 8 * half
        for t in range(rows // 8):
            y = dot(ps[...], lat[pl.ds(t * 8 * cols, 8 * cols), :])
            y = jnp.concatenate([y[:, :full], y[:, full:], y[:, full:]], axis=1).astype(BF)
            ae[pl.ds(half + t * n8, n8), :] = y[:n8]
            nn[pl.ds(t * n8, n8), :] = y[n8 : 2 * n8]
            ss[pl.ds(t * n8, n8), :] = y[2 * n8 :]
        csf[...] = dot(ef[...], ae[pl.ds(half, own), :]).astype(BF)

        start(lat_c)

        def ids(shape, dim, period, width):
            c = lax.broadcasted_iota(jnp.int32, shape, dim)
            c = jnp.where(c >= period, c - period, c)
            s = jnp.zeros(shape, jnp.int32)
            for g in range(1, 5):
                s = s + (c >= bounds[g]).astype(jnp.int32)
            return jnp.where(c < width, s, -1)

        col_id = ids((1, hid), 1, ch, ch)
        row_id = ids((ch, 1), 0, ch, ch)
        same = jnp.where(row_id == col_id, 1.0, 0.0).astype(BF)
        prev = jnp.where(row_id < col_id, 1.0, 0.0).astype(BF)
        for i in ld_w:
            loads[i].wait()
        for d in range(5):
            mask = prev if d == 4 else same
            a = pl.ds(d * full, full)
            wt[a, :] = wt[a, :] * mask[:full]
            b = pl.ds(5 * full + d * rem, rem)
            wt[b, :] = wt[b, :] * mask[full:]
        hid_id = ids((hid, 1), 0, ch, ch)
        par_id = ids((1, 2 * cp), 1, cp, ch)
        omask = jnp.where(hid_id == par_id, 1.0, 0.0).astype(BF)
        loads[ld_ow].wait()
        raw = owr[...].astype(F32)
        pad = jnp.zeros((hid, cp - ch), F32)
        wide = jnp.concatenate([raw[:, :ch], pad, raw[:, ch:], pad], axis=1).astype(BF)
        wo[...] = wide * omask

        loads[ld_hw].wait()
        for i in ld_late:
            loads[i].wait()
        wait_recv(hyper_c)
        taps = dot(tz[...], he[...]).astype(BF)
        hz = jnp.zeros((cells, zch), F32)
        for ab in range(9):
            hz = hz + dot(taps[ab * cells : (ab + 1) * cells], hw[pl.ds(ab * zch, zch), :])
        sz = jax.nn.sigmoid(hz)
        dz = sz * (1.0 + hz * (1.0 - sz))
        f = hz * sz
        feat = jnp.concatenate([jnp.zeros((cells, rem), F32), f[:, 128:], f[:, :128]], axis=1).astype(BF)
        wait_recv(lat_c)

        def mix(even, odd):
            return jnp.concatenate(
                [(even if i % 2 == 0 else odd)[i * half : (i + 1) * half] for i in range(tr)], axis=0)

        lane = lax.broadcasted_iota(jnp.int32, (w, 2 * rem), 1)
        left = lane < rem

        def pair(a, b):
            return jnp.where(left, a, b)

        kidx = lax.broadcasted_iota(jnp.int32, (2 * w, cp), 1)

        def stage_pre(t):
            at = t * w
            a = ae[pl.ds(half + at, w), :]
            au = ae[pl.ds(at, w), :]
            ad = ae[pl.ds(2 * half + at, w), :]
            o = nn[pl.ds(at, w), :]
            s = (ss[pl.ds(at, w), :].astype(F32) + dot(qf[pl.ds(at, w), :], hcf[...])).astype(BF)
            al = mix(a, s)
            ar = mix(s, a)
            hup = dot(up[pl.ds(at, w), :], feat).astype(BF)
            h0, h1 = hup[:, : 2 * rem], hup[:, 2 * rem :]
            x = jnp.concatenate(
                [au[:, :full], ad[:, :full], al[:, :full], ar[:, :full], o[:, :full],
                 pair(au[:, full:], ad[:, full:]), pair(al[:, full:], ar[:, full:]),
                 pair(o[:, full:], h0), h1], axis=1)
            pre_n = dot(x, wt[...])
            xa = jnp.concatenate([pair(a[:, full:], h0), h1], axis=1)
            pre_a = dot(a[:, :full], wt[pl.ds(4 * full, full), :]) + dot(
                xa, wt[pl.ds(5 * full + 4 * rem, rem + zch), :])
            return jnp.concatenate([pre_a, pre_n], axis=0)

        def stage_hidden(pre):
            sg = 0.5 * jnp.tanh(0.5 * pre) + 0.5
            hidden = pre * sg
            return hidden.astype(BF), sg + hidden * (1.0 - sg)

        def stage_nll(t, par):
            at = t * w
            mu = par[:, :cp]
            sraw = par[:, cp:]
            e = jnp.exp(-jnp.abs(sraw))
            e1 = 1.0 + e
            sigma = 0.11 + (jnp.maximum(sraw, 0.0) + jnp.log(e1))
            inv = 1.0 / sigma
            y = jnp.concatenate([ae[pl.ds(half + at, w), :], nn[pl.ds(at, w), :]], axis=0).astype(F32)
            r = (y - mu) * inv
            nll = 0.5 * r * r + jnp.log(sigma)
            rsig = r * inv
            rs[pl.ds(2 * at, 2 * w), :] = rsig
            sgs = jnp.where(sraw >= 0.0, 1.0, e) / e1
            g_par = jnp.concatenate([-rsig, (1.0 - r * r) * inv * sgs], axis=1).astype(BF)
            return nll, g_par

        def stage_rate(t, nll):
            rate = jnp.sum(jnp.where(kidx < ch, nll, 0.0), axis=1, keepdims=True) * (1.0 / ch)
            spread = rate * cm[...].astype(F32)
            hi = spread.astype(BF)
            lo = (spread - hi.astype(F32)).astype(BF)
            rate_v[pl.ds(t * tr, tr), :] = dot(rg[...], hi) + dot(rg[...], lo)

        def stage_gp(t, g_hid, ds):
            at = t * w
            gp = (g_hid * ds).astype(BF)
            ga[pl.ds(at, w), :] = gp[:w]
            gne[pl.ds(half + at, w), :] = gp[w:]
            ut = upt[:, at : at + w]
            return dot(ut, gp[:w]) + dot(ut, gp[w:])

        every = range(tiles)
        pres, hids, pars, nlls, hback, gsums = [], [], [], [], [], []
        for t in every:
            pres.append(stage_pre(t))
        for t in every:
            hids.append(stage_hidden(pres[t]))
            pars.append(dot(hids[t][0], wo[...]))
        for t in every:
            nlls.append(stage_nll(t, pars[t]))
            hback.append(dot_t(nlls[t][1], wo[...]))
        for t in every:
            gsums.append(stage_gp(t, hback[t], hids[t][1]))
        gsum = sum(gsums[1:], gsums[0])

        csb[...] = dot(eb[...], gne[pl.ds(half, own), :]).astype(BF)
        start(gpre_c)

        hi = gsum.astype(BF)
        lo = (gsum - hi.astype(F32)).astype(BF)
        both = jnp.concatenate([hi, lo], axis=0)
        p0 = dot_t(both, wt[pl.ds(5 * ch + zch - 128, 128), :])
        p1 = dot_t(both, wt[pl.ds(5 * ch, zch - 128), :])
        g_h = jnp.concatenate([p0[:cells] + p0[cells:], p1[:cells] + p1[cells:]], axis=1)
        g_hz = (g_h * dz).astype(BF)
        gz[pl.ds(0, cells), :] = g_hz
        csz[...] = dot(ez[...], g_hz).astype(BF)
        start(gz_c)

        def main_w(d):
            return wt[pl.ds(d * full, full), :]

        def rest_w(d):
            return wt[pl.ds(5 * full + d * rem, rem), :]

        shifts, vns = [], []
        for t in every:
            at = t * w
            gn = gne[pl.ds(half + at, w), :]
            shifts.append(dot(sb[...], gn))
            nm = rs[pl.ds(2 * at + w, w), :full] + dot_t(gn, main_w(4))
            nq = rs[pl.ds(2 * at + w, w), full:ch] + dot_t(gn, rest_w(4))
            vns.append(jnp.concatenate([nm, nq], axis=1).astype(BF))
            gs = ga[pl.ds(at, w), :]
            m = rs[pl.ds(2 * at, w), :full] + dot_t(gs, main_w(4))
            q = rs[pl.ds(2 * at, w), full:ch] + dot_t(gs, rest_w(4))
            rs[pl.ds(2 * at, w), :full] = m
            rs[pl.ds(2 * at, w), full:ch] = q
            stage_rate(t, nlls[t][0])
        rate_copy = pltpu.make_async_copy(rate_v, rate_out, out_sem.at[0])
        rate_copy.start()

        wait_recv(gpre_c)
        outs = [rate_copy]
        for t in every:
            at = t * w
            gn = gne[pl.ds(half + at, w), :]
            gu = gne[pl.ds(at, w), :]
            gd = gne[pl.ds(2 * half + at, w), :]
            s = (shifts[t] + dot(qb[pl.ds(at, w), :], hcb[...])).astype(BF)
            gs = (gd, gu, mix(gn, s), mix(s, gn))
            m = rs[pl.ds(2 * at, w), :full]
            q = rs[pl.ds(2 * at, w), full:ch]
            for d in range(4):
                m = m + dot_t(gs[d], main_w(d))
                q = q + dot_t(gs[d], rest_w(d))
            va = jnp.concatenate([m, q], axis=1).astype(BF)
            vn = vns[t]
            for u in range(tr // 8):
                v = jnp.concatenate([va[u * n8 : (u + 1) * n8], vn[u * n8 : (u + 1) * n8]], axis=0)
                gl_v[pl.ds((t * tr + u * 8) * cols, 8 * cols), :] = dot(pt[...], v).astype(BF)
            span = pl.ds(t * tr * cols, tr * cols)
            c = pltpu.make_async_copy(gl_v.at[span], gl_out.at[span], out_sem.at[2 + t])
            c.start()
            outs.append(c)

        wait_recv(gz_c)
        taps = dot(tz[...], gz[...]).astype(BF)
        acc = jnp.zeros((cells, zch), F32)
        for ab in range(9):
            back = 8 - ab
            acc = acc + dot_t(taps[back * cells : (back + 1) * cells], hw[pl.ds(ab * zch, zch), :])
        gh_v[...] = acc
        c = pltpu.make_async_copy(gh_v, gh_out, out_sem.at[1])
        c.start()
        outs.append(c)
        for c in outs:
            c.wait()

        wait_send(hyper_c)
        wait_send(lat_c)
        wait_send(gpre_c)
        wait_send(gz_c)

    return kernel


def move(rate, gl, gh, rate_out, gl_out, gh_out, rate_v, gl_v, gh_v, sem, sem_out):
    parts = 4
    size = gl.shape[0] // parts
    triples = [(rate, rate_v, rate_out), (gh, gh_v, gh_out)]
    for i in range(parts):
        span = pl.ds(i * size, size)
        triples.append((gl.at[span], gl_v.at[span], gl_out.at[span]))
    ins = [pltpu.make_async_copy(a, b, sem.at[i]) for i, (a, b, _) in enumerate(triples)]
    outs = [pltpu.make_async_copy(b, c, sem_out.at[i]) for i, (_, b, c) in enumerate(triples)]
    for c in ins:
        c.start()
    for a, b in zip(ins, outs):
        a.wait()
        b.start()
    for c in outs:
        c.wait()


def finish(*arrays):
    anyspec = pl.BlockSpec(memory_space=pl.ANY)
    return pl.pallas_call(
        move,
        out_shape=tuple(jax.ShapeDtypeStruct(a.shape, a.dtype) for a in arrays),
        in_specs=[anyspec] * 3,
        out_specs=(anyspec,) * 3,
        scratch_shapes=[pltpu.VMEM(a.shape, a.dtype) for a in arrays] + [pltpu.SemaphoreType.DMA((6,))] * 2,
    )(*arrays)


def solution(mesh):
    nrow, ncol = mesh.shape["row"], mesh.shape["col"]

    def local(latent, hyper, bounds, hyper_weight, prior_weight, ctx_weight, chan_weight, out_weight):
        rows, cols, ch = latent.shape
        zrows, zcols, zch = hyper.shape
        hid = prior_weight.shape[1]
        tr = 16
        half = cols // 2
        full = (ch // 256) * 256
        rem = ch - full
        cp = full + 2 * rem
        cells = zrows * zcols
        own = rows * half
        tabs = tables(rows, cols, zrows, zcols, tr)
        hr = rows // 2
        anyspec = pl.BlockSpec(memory_space=pl.ANY)
        v = lambda *s, dt=BF: pltpu.VMEM(s, dt)
        scratch = [
            v(rows * cols, ch), v(9 * zch, zch), v(5 * ch + zch, hid), v(hid, hid), v(hid, 2 * cp),
            *[v(*t.shape) for t in tabs],
            v(own + 2 * half, cp), v(own, cp), v(own, cp), v(2 * hr, cp), v(2 * hr, cp),
            v(cells + 128, zch), v(32, zch),
            v(own + 2 * half, hid), v(own, hid), v(rows * cols, cp, dt=F32), v(2 * hr, hid), v(2 * hr, hid),
            v(cells + 128, zch), v(32, zch),
            v(rows, cols, dt=F32), v(rows * cols, ch), v(cells, zch, dt=F32),
            pltpu.SemaphoreType.DMA((32,)), pltpu.SemaphoreType.DMA((2 + rows // tr,)), pltpu.SemaphoreType.DMA((24,)), pltpu.SemaphoreType.DMA((24,)),
        ]
        rate, gl, gh = pl.pallas_call(
            make_kernel(rows, cols, ch, zrows, zcols, zch, hid, tr, nrow, ncol),
            out_shape=(
                jax.ShapeDtypeStruct((rows, cols), F32),
                jax.ShapeDtypeStruct((rows * cols, ch), BF),
                jax.ShapeDtypeStruct((cells, zch), F32),
            ),
            in_specs=[pl.BlockSpec(memory_space=pltpu.SMEM)] + [anyspec] * (7 + len(tabs)),
            out_specs=(anyspec, anyspec, anyspec),
            scratch_shapes=scratch,
            compiler_params=pltpu.CompilerParams(
                collective_id=0, has_side_effects=True, vmem_limit_bytes=56 * 1024 * 1024),
        )(
            bounds, latent.reshape(rows * cols, ch), hyper.reshape(cells, zch),
            hyper_weight.reshape(9 * zch, zch), prior_weight, ctx_weight.reshape(4 * ch, hid),
            chan_weight, out_weight, *[jnp.asarray(t) for t in tabs],
        )
        rate, gl, gh = finish(rate, gl, gh)
        return rate, gl.reshape(rows, cols, ch), gh.reshape(zrows, zcols, zch)

    in_specs = (
        P(("parts", "row"), "col", None),
        P(("parts", "row"), "col", None),
        P(),
        P(),
        P(),
        P(),
        P(),
        P(),
    )
    out_specs = (
        P(("parts", "row"), "col"),
        P(("parts", "row"), "col", None),
        P(("parts", "row"), "col", None),
    )
    return jax.shard_map(local, mesh=mesh, in_specs=in_specs, out_specs=out_specs, check_vma=False)
```
